256 devices in a mesh: store: 32 (over z, x), head: 8 (over y, core).
Axes of the slice: x: 4, y: 4, z: 8, core: 2. Of those that a mesh axis runs over, the one named last changes fastest.
Arguments:
- queries: bfloat16 [2048, 8192], P('store', 'head'), may hold values from -16 to 16
- suffix_kv: bfloat16 [2048, 8, 256], P('store', 'head'), may hold values from -6 to 6
- kv_cache: bfloat16 [4096, 8, 64, 256], P('store', 'head'), may hold values from -16 to 16
- block_owner: int32 [32, 128], P('store'), may hold values from 0 to 31, as said below
- block_slot: int32 [32, 128], P('store'), may hold values from 0 to 127, as said below
- prefix_blocks: int32 [32], P('store'), may hold values from 1 to 128, as said below
- out_weight: bfloat16 [8192, 4096], P('head'), may hold values from -0.0625 to 0.0625
Outputs:
- projected: bfloat16 [2048, 4096], P(('store', 'head'))
The draws below stay inside these ranges and needn't reach their ends.
Inputs may be any that keep to these rules, and one draw needn't show every extreme that they name: `block_owner`: entries j < prefix_blocks of a request name the owners of its cached blocks; a request has at most 4 live blocks at one owner, and some request has exactly 4 at every owner; later entries are arbitrary. `block_slot`: slot of each block at its owner; the live entries of all requests name distinct owner and slot pairs. `prefix_blocks`: the largest equals 128.
All inputs are finite; a program needn't handle non-finite values.
Results may differ from the reference program's by a relative error of at most 0.022.
Values may be sent and summed in bfloat16 or wider, within the bound.
No kernel may reach another device: no remote copies, remote signals or barrier semaphores. Data moves between devices by JAX's collectives and lax.ppermute only.
A program may use at most 128 MiB of HBM per device.

```python
import jax
import jax.numpy as jnp
from jax import lax

HEADS = 64
KV_HEADS = 8
HD = 128
DO = 4096
SUF = 64
BLK = 64
CAP = 4
GROUP = 8
REQUESTS = 32
SLOTS = 128
MAXB = 128
N_STORE = 32


def block_layout(key):
    key = jax.random.fold_in(key, 101)
    keys = jax.random.split(key, 5)
    homes = jnp.arange(REQUESTS)
    widest = jax.random.randint(keys[0], (), 0, REQUESTS)
    home_cap = jax.random.randint(keys[1], (REQUESTS,), 1, CAP + 1)
    home_cap = jnp.where(homes == widest, CAP, home_cap)
    lowest = (home_cap + 1) // 2
    counts = jax.random.randint(keys[2], (REQUESTS, N_STORE), lowest[:, None], home_cap[:, None] + 1)
    counts = jnp.where((homes == widest)[:, None], CAP, counts)
    entry = jnp.arange(MAXB)
    owner_of = entry // CAP
    depth = entry % CAP
    usable = depth[None, :] < jnp.take(counts, owner_of, axis=1)
    shuffles = jax.vmap(lambda item: jax.random.permutation(item, MAXB))(jax.random.split(keys[3], REQUESTS))
    priority = jnp.where(usable, 0, MAXB) + shuffles
    ordering = jnp.argsort(priority, axis=1)
    owners = (ordering // CAP).astype(jnp.int32)
    depths = (ordering % CAP).astype(jnp.int32)
    slot_tables = jax.vmap(lambda item: jax.random.permutation(item, SLOTS))(jax.random.split(keys[4], N_STORE))
    slots = slot_tables[owners, homes[:, None] * CAP + depths]
    lengths = jnp.sum(counts, axis=1)
    return (owners, slots.astype(jnp.int32), lengths.astype(jnp.int32))


def draw_block_owner(key, part):
    shared = block_layout(key)
    return shared[0]


def draw_block_slot(key, part):
    shared = block_layout(key)
    return shared[1]


def draw_prefix_blocks(key, part):
    shared = block_layout(key)
    return shared[2]


def draw_queries(key, part):
    key = jax.random.fold_in(key, 2)
    first_key = jax.random.fold_in(key, 0)
    values = jnp.clip(jax.random.normal(first_key, (REQUESTS * SUF, KV_HEADS, GROUP, HD), jnp.float32), -6.0, 6.0)
    return jnp.clip(values, -16.0, 16.0).reshape(REQUESTS * SUF, HEADS * HD).astype(jnp.bfloat16)


def draw_kv_cache(key, part):
    key = jax.random.fold_in(key, 3)
    first_key = jax.random.fold_in(key, 0)
    values = jnp.clip(jax.random.normal(first_key, (N_STORE * SLOTS, KV_HEADS, BLK, 2 * HD), jnp.float32), -6.0, 6.0)
    return jnp.clip(values, -16.0, 16.0).astype(jnp.bfloat16)


def block_scale(rng, shape, cuts, low, top_value):
    def one(dim, shards_of):
        draws = jax.random.uniform(jax.random.fold_in(jax.random.fold_in(rng, 6), dim), (shards_of,), jnp.float32, low / len(cuts), top_value / len(cuts))
        return jnp.repeat(jnp.exp(draws), shape[dim] // shards_of).reshape((-1,) + (1,) * (len(shape) - dim - 1))

    factor_of = one(*cuts[0])
    for cut in cuts[1:]:
        factor_of = factor_of * one(*cut)
    return factor_of


def centred(own_key, dims, scale, reach, pieces=(), kind=jnp.bfloat16):
    gain = block_scale(own_key, dims, pieces, -0.22, 0.18) if pieces else 1.0
    entries = jax.random.normal(own_key, dims, jnp.float32) * scale * gain
    return jnp.minimum(jnp.maximum(entries, -reach), reach).astype(kind)


def setup_inputs(seed: int = 0) -> dict:
    streams_of = jax.random.split(jax.random.key(seed), 8)
    return {
        "queries": draw_queries(jax.random.fold_in(streams_of[7], 71), 0),
        "suffix_kv": centred(streams_of[1], (REQUESTS * SUF, KV_HEADS, 2 * HD), 1.0, 6.0, ((0, 32), (1, 8))),
        "kv_cache": draw_kv_cache(jax.random.fold_in(streams_of[7], 71), 0),
        "block_owner": draw_block_owner(jax.random.fold_in(streams_of[7], 71), 0),
        "block_slot": draw_block_slot(jax.random.fold_in(streams_of[7], 71), 0),
        "prefix_blocks": draw_prefix_blocks(jax.random.fold_in(streams_of[7], 71), 0),
        "out_weight": centred(streams_of[6], (HEADS * HD, DO), (HEADS * HD) ** -0.5, 0.0625, ((0, 8),)),
    }


NEG_FILL = -1.0e30


def attend_request(index, queries, suffix_kv, kv_cache, block_owner, block_slot, prefix_blocks):
    inv_root = HD ** -0.5
    query_block = lax.dynamic_slice_in_dim(queries, index * SUF, SUF, 0).astype(jnp.float32).reshape(SUF, KV_HEADS, GROUP, HD)
    row_ids = (block_owner[index] * SLOTS + block_slot[index]).astype(jnp.int32)
    cached = kv_cache[row_ids].astype(jnp.float32).transpose(1, 0, 2, 3).reshape(KV_HEADS, MAXB * BLK, 2 * HD)
    suffix_part = lax.dynamic_slice_in_dim(suffix_kv, index * SUF, SUF, 0).astype(jnp.float32).transpose(1, 0, 2)
    key_rows = jnp.concatenate([cached, suffix_part], axis=1)
    in_prefix = jnp.repeat(jnp.arange(MAXB) < prefix_blocks[index], BLK)
    causal = jnp.arange(SUF)[None, :] <= jnp.arange(SUF)[:, None]
    visible = jnp.concatenate([jnp.broadcast_to(in_prefix[None, :], (SUF, MAXB * BLK)), causal], axis=1)
    scores = jnp.einsum("tgid,gkd->gtik", query_block, key_rows[:, :, :HD]) * inv_root
    mask = visible[None, :, None, :]
    masked = jnp.where(mask, scores, NEG_FILL)
    row_peak = jnp.max(masked, axis=3, keepdims=True)
    expo = jnp.where(mask, jnp.exp(masked - row_peak), 0.0)
    row_sum = jnp.sum(expo, axis=3)
    rounded = lax.optimization_barrier(expo.astype(jnp.bfloat16)).astype(jnp.float32)
    summed = jnp.einsum("gtik,gkd->gtid", rounded, key_rows[:, :, HD:])
    attended = (summed / row_sum[..., None]).astype(jnp.bfloat16)
    return attended.transpose(1, 0, 2, 3).reshape(SUF, HEADS * HD)


def reference(queries, suffix_kv, kv_cache, block_owner, block_slot, prefix_blocks, out_weight):
    def one_request(index):
        return attend_request(index, queries, suffix_kv, kv_cache, block_owner, block_slot, prefix_blocks)

    attended = lax.map(one_request, jnp.arange(REQUESTS, dtype=jnp.int32)).reshape(REQUESTS * SUF, HEADS * HD)
    return jnp.dot(attended, out_weight, preferred_element_type=jnp.float32).astype(jnp.bfloat16)
```

```python
import functools
import math

import jax
import jax.numpy as jnp
from jax import lax
from jax.experimental import pallas as pl
from jax.experimental.pallas import tpu as pltpu
from jax.sharding import PartitionSpec as P

HD = 128
SUF = 64
BLK = 64
CAP = 4
GROUP = 8
ROWS = SUF * GROUP
STATS = 16
PACKET = HD + STATS
NX = 4
NZ = 8
NY = 4
CORES = 2

NEG_FILL = -1e30
FLOOR = -1e9
TO_LOG2 = math.log2(math.e) / math.sqrt(HD)
CHUNKS = ((4, 3, 5), (2, 6), (1, 7), (0,))
VMEM_LIMIT = 32 * 1024 * 1024

CONTRACT_LAST = (((1,), (1,)), ((), ()))
CONTRACT_FIRST = (((0,), (0,)), ((), ()))


def rem(a, n):
    return lax.rem(a + n, n)


def pick_kernel(shifts, place_ref, table_ref, cache_ref, *rest):
    outs, sems = rest[:NX], rest[NX]
    zo, xo = place_ref[0], place_ref[1]
    me = zo * NX + xo
    for k in range(NX):
        xr = rem(xo + k, NX)
        for n, shift in enumerate(shifts):
            home = rem(zo + shift, NZ) * NX + xr
            for c in range(CAP):
                slot = jnp.clip(table_ref[home, me * CAP + c], 0, cache_ref.shape[0] - 1)
                pltpu.make_async_copy(
                    cache_ref.at[pl.ds(slot, 1)],
                    outs[k].at[pl.ds(n * CAP + c, 1)],
                    sems.at[k],
                ).start()
    for k in range(NX):
        pltpu.make_async_copy(cache_ref.at[pl.ds(0, len(shifts) * CAP)], outs[k], sems.at[k]).wait()


def pick(shifts, place, table, cache):
    shape = jax.ShapeDtypeStruct((len(shifts) * CAP, BLK, 2 * HD), cache.dtype)
    return pl.pallas_call(
        functools.partial(pick_kernel, shifts),
        out_shape=[shape] * NX,
        in_specs=[
            pl.BlockSpec(memory_space=pltpu.SMEM),
            pl.BlockSpec(memory_space=pltpu.SMEM),
            pl.BlockSpec(memory_space=pl.ANY),
        ],
        out_specs=[pl.BlockSpec(memory_space=pl.ANY)] * NX,
        scratch_shapes=[pltpu.SemaphoreType.DMA((NX,))],
        compiler_params=pltpu.CompilerParams(vmem_limit_bytes=VMEM_LIMIT),
        name="pick_blocks",
    )(place, table, cache)


def head_rows(block):
    return jnp.concatenate([block[:, i * HD : (i + 1) * HD] for i in range(GROUP)], axis=0)


def partial_packet(score_parts, value_parts):
    peak = functools.reduce(
        jnp.maximum, [jnp.max(part, axis=0, keepdims=True) for part in score_parts]
    )
    shift = jnp.maximum(peak * TO_LOG2, FLOOR).astype(jnp.bfloat16).astype(jnp.float32)
    total = jnp.zeros((1, ROWS), jnp.float32)
    acc = jnp.zeros((HD, ROWS), jnp.float32)
    for part, values in zip(score_parts, value_parts):
        expo = jnp.exp2(part * TO_LOG2 - shift)
        total += jnp.sum(expo, axis=0, keepdims=True)
        acc += lax.dot_general(
            values, expo.astype(jnp.bfloat16), CONTRACT_FIRST, preferred_element_type=jnp.float32
        )
    high = total.astype(jnp.bfloat16).astype(jnp.float32)
    line = lax.broadcasted_iota(jnp.int32, (STATS, ROWS), 0)
    stats = jnp.where(line == 0, shift, jnp.where(line == 1, high, jnp.where(line == 2, total - high, 0.0)))
    return acc.astype(jnp.bfloat16), stats.astype(jnp.bfloat16)


def attend_kernel(shifts, place_ref, table_ref, query_ref, *rest):
    blocks, outs = rest[:NX], rest[NX:]
    zo, xr = place_ref[0], place_ref[1]
    for n, shift in enumerate(shifts):
        zr = rem(zo + shift, NZ)
        rows = head_rows(query_ref[pl.ds(zr * SUF, SUF), :])
        score_parts, value_parts = [], []
        for k in range(NX):
            owner = zo * NX + rem(xr - k, NX)
            both = blocks[k][n * CAP : (n + 1) * CAP].reshape(CAP * BLK, 2 * HD)
            scores = lax.dot_general(
                both[:, :HD], rows, CONTRACT_LAST, preferred_element_type=jnp.float32
            )
            live = [
                jnp.where(
                    table_ref[zr * NX + xr, owner * CAP + c] >= 0,
                    scores[c * BLK : (c + 1) * BLK],
                    NEG_FILL,
                )
                for c in range(CAP)
            ]
            score_parts.append(jnp.concatenate(live, axis=0))
            value_parts.append(both[:, HD:])
        acc, stats = partial_packet(score_parts, value_parts)
        outs[n][:HD, :] = acc
        outs[n][HD:, :] = stats


def attend(shifts, place, table, queries, blocks):
    keys = len(shifts) * NX * CAP * BLK
    return pl.pallas_call(
        functools.partial(attend_kernel, shifts),
        out_shape=[jax.ShapeDtypeStruct((PACKET, ROWS), jnp.bfloat16)] * len(shifts),
        in_specs=[pl.BlockSpec(memory_space=pltpu.SMEM)] * 2
        + [pl.BlockSpec(memory_space=pltpu.VMEM)] * (1 + NX),
        out_specs=[pl.BlockSpec(memory_space=pltpu.VMEM)] * len(shifts),
        compiler_params=pltpu.CompilerParams(vmem_limit_bytes=VMEM_LIMIT),
        cost_estimate=pl.CostEstimate(
            flops=4 * keys * ROWS * HD, bytes_accessed=4 * keys * HD, transcendentals=keys * ROWS
        ),
        name="attend_chunk",
    )(place, table, queries, *blocks)


def own_kernel(query_ref, suffix_ref, out_ref):
    rows = head_rows(query_ref[...])
    both = suffix_ref[...]
    scores = lax.dot_general(both[:, :HD], rows, CONTRACT_LAST, preferred_element_type=jnp.float32)
    key = lax.broadcasted_iota(jnp.int32, (SUF, ROWS), 0)
    token = lax.rem(lax.broadcasted_iota(jnp.int32, (SUF, ROWS), 1), SUF)
    acc, stats = partial_packet([jnp.where(key <= token, scores, NEG_FILL)], [both[:, HD:]])
    out_ref[:HD, :] = acc
    out_ref[HD:, :] = stats


def own_part(queries, suffix):
    return pl.pallas_call(
        own_kernel,
        out_shape=jax.ShapeDtypeStruct((PACKET, ROWS), jnp.bfloat16),
        compiler_params=pltpu.CompilerParams(vmem_limit_bytes=VMEM_LIMIT),
        name="attend_suffix",
    )(queries, suffix)


def project_kernel(*refs):
    packets, weight_ref, out_ref = refs[:-2], refs[-2], refs[-1]
    stats = [ref[HD:, :].astype(jnp.float32) for ref in packets]
    top = functools.reduce(jnp.maximum, [s[0:1] for s in stats])
    factors = [jnp.exp2(s[0:1] - top) for s in stats]
    row_sum = sum(f * (s[1:2] + s[2:3]) for f, s in zip(factors, stats))
    summed = sum(f * ref[:HD, :].astype(jnp.float32) for f, ref in zip(factors, packets))
    rows = (summed / row_sum).T.astype(jnp.bfloat16)
    attended = jnp.concatenate([rows[i * SUF : (i + 1) * SUF] for i in range(GROUP)], axis=1)
    out_ref[...] = jnp.dot(
        attended, weight_ref[...], preferred_element_type=jnp.float32
    ).astype(jnp.bfloat16)


def project(packets, weight):
    return pl.pallas_call(
        project_kernel,
        out_shape=jax.ShapeDtypeStruct((SUF, weight.shape[1]), jnp.bfloat16),
        compiler_params=pltpu.CompilerParams(vmem_limit_bytes=VMEM_LIMIT),
        cost_estimate=pl.CostEstimate(
            flops=2 * SUF * weight.size, bytes_accessed=2 * weight.size, transcendentals=0
        ),
        name="merge_project",
    )(*packets, weight)


def x_permute(a, step):
    pairs = [
        (z * NX + x, z * NX + (x + step) % NX) for z in range(NZ) for x in range(NX)
    ]
    return lax.ppermute(a, "store", pairs)


def z_permute(a, step):
    pairs = [
        (z * NX + x, ((z + step) % NZ) * NX + x) for z in range(NZ) for x in range(NX)
    ]
    return lax.ppermute(a, "store", pairs)


def y_permute(a, step):
    pairs = [
        (y * CORES + c, ((y + step) % NY) * CORES + c) for y in range(NY) for c in range(CORES)
    ]
    return lax.ppermute(a, "head", pairs)


def core_swap(a):
    return lax.ppermute(a, "head", [(h, h ^ 1) for h in range(NY * CORES)])


def sum_heads(partial):
    core = lax.rem(lax.axis_index("head"), CORES)
    y = lax.axis_index("head") // CORES
    parts = partial.reshape(NY, CORES, SUF // (NY * CORES), partial.shape[1])
    pick_core = lambda which: lax.dynamic_index_in_dim(parts, which, 1, keepdims=False)
    other = core_swap(pick_core(1 - core))
    both = pick_core(core).astype(jnp.float32) + other.astype(jnp.float32)
    pick_y = lambda step: lax.dynamic_index_in_dim(both, rem(y + step, NY), 0, keepdims=False)
    arrived = [y_permute(pick_y(step).astype(jnp.bfloat16), step) for step in (2, 1, 3)]
    return (pick_y(0) + sum(a.astype(jnp.float32) for a in arrived)).astype(jnp.bfloat16)


def local(queries, suffix_kv, kv_cache, block_owner, block_slot, prefix_blocks, out_weight):
    store_count = lax.axis_size("store")
    me = lax.axis_index("store")
    place = jnp.stack([me // NX, lax.rem(me, NX)]).astype(jnp.int32)
    owner_list = block_owner[0]
    slot_list = block_slot[0]
    in_prefix = jnp.arange(owner_list.shape[0]) < prefix_blocks[0]
    at_owner = (owner_list[:, None] == jnp.arange(store_count)[None, :]) & in_prefix[:, None]
    ordinal = jnp.cumsum(at_owner.astype(jnp.int32), axis=0) - 1
    placed = at_owner[:, :, None] & (ordinal[:, :, None] == jnp.arange(CAP)[None, None, :])
    wanted = jnp.sum(jnp.where(placed, slot_list[:, None, None] + 1, 0), axis=0) - 1
    copies = jnp.broadcast_to(wanted.reshape(1, -1), (store_count, store_count * CAP))
    table = lax.all_to_all(copies, "store", split_axis=0, concat_axis=0, tiled=True)
    z_groups = [[z * NX + x for z in range(NZ)] for x in range(NX)]
    z_queries = lax.all_gather(queries, "store", axis=0, tiled=True, axis_index_groups=z_groups)
    cache = kv_cache.reshape(kv_cache.shape[0], BLK, 2 * HD)
    own = own_part(queries, suffix_kv.reshape(SUF, 2 * HD))
    packets = []
    for shifts in CHUNKS:
        picked = pick(shifts, place, table, cache)
        blocks = [picked[0]] + [x_permute(picked[k], k) for k in range(1, NX)]
        for shift, packet in zip(shifts, attend(shifts, place, table, z_queries, blocks)):
            packets.append(z_permute(packet, shift) if shift else packet)
    return sum_heads(project(packets + [own], out_weight))


def solution(mesh):
    in_specs = (
        P("store", "head"),
        P("store", "head", None),
        P("store", "head", None, None),
        P("store", None),
        P("store", None),
        P("store"),
        P("head", None),
    )
    out_specs = P(("store", "head"), None)
    return jax.shard_map(local, mesh=mesh, in_specs=in_specs, out_specs=out_specs, check_vma=False)
```

```python
import functools
import math

import jax
import jax.numpy as jnp
from jax import lax
from jax.experimental import pallas as pl
from jax.experimental.pallas import tpu as pltpu
from jax.sharding import PartitionSpec as P

HD = 128
SUF = 64
BLK = 64
CAP = 4
GROUP = 8
ROWS = SUF * GROUP
STATS = 16
PACKET = HD + STATS
NX = 4
NZ = 8
NY = 4
CORES = 2
HEAD_ROWS = SUF // (NY * CORES)

NEG_FILL = -1e30
FLOOR = -1e9
TO_LOG2 = math.log2(math.e) / math.sqrt(HD)
CHUNKS = ((4, 3, 5, 2), (6, 7, 1), (0,))
AHEAD = 2
VMEM_LIMIT = 40 * 1024 * 1024

CONTRACT_LAST = (((1,), (1,)), ((), ()))
CONTRACT_FIRST = (((0,), (0,)), ((), ()))

IN_SMEM = pl.BlockSpec(memory_space=pltpu.SMEM)
IN_VMEM = pl.BlockSpec(memory_space=pltpu.VMEM)
IN_HBM = pl.BlockSpec(memory_space=pltpu.HBM)


def keep_in_hbm(a):
    return pltpu.with_memory_space_constraint(a, pltpu.HBM)


def rem(a, n):
    return lax.rem(a + n, n)


def coordinates(me_ref):
    return lax.div(me_ref[0], NX), lax.rem(me_ref[0], NX)


def wanted_kernel(length_ref, owner_ref, slot_ref, out_ref):
    count = owner_ref.shape[1]
    owners = count // CAP
    entry = lax.broadcasted_iota(jnp.int32, (1, count), 1)
    owner = jnp.where(entry < length_ref[0], owner_ref[...], owners)
    at_owner = lax.broadcasted_iota(jnp.int32, (owners, count), 0) == owner
    hits = jnp.where(at_owner, 1.0, 0.0)
    earlier = lax.broadcasted_iota(jnp.int32, (count, count), 0) < lax.broadcasted_iota(
        jnp.int32, (count, count), 1
    )
    before = jnp.dot(
        hits.astype(jnp.bfloat16),
        jnp.where(earlier, 1.0, 0.0).astype(jnp.bfloat16),
        preferred_element_type=jnp.float32,
    )
    ordinal = jnp.sum(before * hits, axis=0, keepdims=True).astype(jnp.int32)
    target = jnp.where(ordinal < CAP, owner * CAP + ordinal, count)
    chosen = jnp.where(lax.broadcasted_iota(jnp.int32, (count, count), 0) == target, 1.0, 0.0)
    slots = jnp.broadcast_to((slot_ref[...] + 1).astype(jnp.float32), (8, count))
    row = lax.dot_general(
        slots.astype(jnp.bfloat16),
        chosen.astype(jnp.bfloat16),
        CONTRACT_LAST,
        preferred_element_type=jnp.float32,
    )
    out_ref[...] = jnp.broadcast_to(
        (row[0:1].astype(jnp.int32) - 1).reshape(1, 1, count), out_ref.shape
    )


def wanted_slots(prefix_blocks, block_owner, block_slot, store_count):
    return pl.pallas_call(
        wanted_kernel,
        out_shape=jax.ShapeDtypeStruct((store_count, 1, block_owner.shape[1]), jnp.int32),
        in_specs=[IN_SMEM, IN_VMEM, IN_VMEM],
        out_specs=IN_VMEM,
        compiler_params=pltpu.CompilerParams(vmem_limit_bytes=VMEM_LIMIT),
        name="wanted_slots",
    )(prefix_blocks, block_owner, block_slot)


def slot_of(table_ref, home, owner, c, cache_ref):
    return jnp.clip(table_ref[home, 0, owner * CAP + c], 0, cache_ref.shape[0] - 1)


def start_picks(shifts, me_ref, table_ref, cache_ref, outs, sems):
    zo, xo = coordinates(me_ref)
    for k in range(1, NX):
        for n, shift in enumerate(shifts):
            home = rem(zo + shift, NZ) * NX + rem(xo + k, NX)
            for c in range(CAP):
                slot = slot_of(table_ref, home, me_ref[0], c, cache_ref)
                pltpu.make_async_copy(
                    cache_ref.at[pl.ds(slot, 1)],
                    outs[k - 1].at[pl.ds(n * CAP + c, 1)],
                    sems.at[k - 1],
                ).start()


def wait_picks(shifts, cache_ref, outs, sems):
    for k in range(1, NX):
        pltpu.make_async_copy(
            cache_ref.at[pl.ds(0, len(shifts) * CAP)], outs[k - 1], sems.at[k - 1]
        ).wait()


def start_own_blocks(shifts, me_ref, table_ref, cache_ref, here_ref, sem):
    zo, xo = coordinates(me_ref)
    for n, shift in enumerate(shifts):
        for c in range(CAP):
            slot = slot_of(table_ref, rem(zo + shift, NZ) * NX + xo, me_ref[0], c, cache_ref)
            pltpu.make_async_copy(
                cache_ref.at[pl.ds(slot, 1)], here_ref.at[pl.ds(n * CAP + c, 1)], sem
            ).start()


def wait_own_blocks(shifts, cache_ref, here_ref, sem):
    pltpu.make_async_copy(cache_ref.at[pl.ds(0, len(shifts) * CAP)], here_ref, sem).wait()


def picked_shapes(shifts, dtype):
    return [jax.ShapeDtypeStruct((len(shifts) * CAP, BLK, 2 * HD), dtype)] * (NX - 1)


def pick_kernel(shifts, me_ref, table_ref, cache_ref, *rest):
    outs, sems = rest[:-1], rest[-1]
    start_picks(shifts, me_ref, table_ref, cache_ref, outs, sems)
    wait_picks(shifts, cache_ref, outs, sems)


def pick(shifts, me, table, cache):
    shapes = picked_shapes(shifts, cache.dtype)
    return pl.pallas_call(
        functools.partial(pick_kernel, shifts),
        out_shape=shapes,
        in_specs=[IN_SMEM, IN_SMEM, IN_HBM],
        out_specs=[IN_HBM] * len(shapes),
        scratch_shapes=[pltpu.SemaphoreType.DMA((NX - 1,))],
        compiler_params=pltpu.CompilerParams(vmem_limit_bytes=VMEM_LIMIT),
        name="pick_blocks",
    )(me, table, cache)


def head_rows(block):
    return jnp.concatenate([block[:, i * HD : (i + 1) * HD] for i in range(GROUP)], axis=0)


def partial_sums(score_parts, value_parts):
    peak = functools.reduce(
        jnp.maximum, [jnp.max(part, axis=0, keepdims=True) for part in score_parts]
    )
    shift = jnp.maximum(peak * TO_LOG2, FLOOR).astype(jnp.bfloat16).astype(jnp.float32)
    total = jnp.zeros((1, ROWS), jnp.float32)
    acc = jnp.zeros((HD, ROWS), jnp.float32)
    for part, values in zip(score_parts, value_parts):
        expo = jnp.exp2(part * TO_LOG2 - shift)
        total += jnp.sum(expo, axis=0, keepdims=True)
        acc += lax.dot_general(
            values, expo.astype(jnp.bfloat16), CONTRACT_FIRST, preferred_element_type=jnp.float32
        )
    return shift, total, acc


def write_packet(out_ref, shift, total, acc):
    high = total.astype(jnp.bfloat16).astype(jnp.float32)
    line = lax.broadcasted_iota(jnp.int32, (STATS, ROWS), 0)
    stats = jnp.where(line == 0, shift, jnp.where(line == 1, high, jnp.where(line == 2, total - high, 0.0)))
    out_ref[:HD, :] = acc.astype(jnp.bfloat16)
    out_ref[HD:, :] = stats.astype(jnp.bfloat16)


def read_packet(ref):
    stats = ref[HD:, :].astype(jnp.float32)
    return stats[0:1], stats[1:2] + stats[2:3], ref[:HD, :].astype(jnp.float32)


def cached_part(shift, n, me_ref, table_ref, rows, blocks):
    zo, xr = coordinates(me_ref)
    home = rem(zo + shift, NZ) * NX + xr
    score_parts, value_parts = [], []
    for k in (1, 2, 3, 0):
        owner = zo * NX + rem(xr - k, NX)
        both = blocks[k][n * CAP : (n + 1) * CAP].reshape(CAP * BLK, 2 * HD)
        scores = lax.dot_general(both[:, :HD], rows, CONTRACT_LAST, preferred_element_type=jnp.float32)
        live = [
            jnp.where(
                table_ref[home, 0, owner * CAP + c] >= 0,
                scores[c * BLK : (c + 1) * BLK],
                NEG_FILL,
            )
            for c in range(CAP)
        ]
        score_parts.append(jnp.concatenate(live, axis=0))
        value_parts.append(both[:, HD:])
    return partial_sums(score_parts, value_parts)


def suffix_part(rows, both):
    scores = lax.dot_general(both[:, :HD], rows, CONTRACT_LAST, preferred_element_type=jnp.float32)
    key = lax.broadcasted_iota(jnp.int32, (SUF, ROWS), 0)
    token = lax.rem(lax.broadcasted_iota(jnp.int32, (SUF, ROWS), 1), SUF)
    return partial_sums([jnp.where(key <= token, scores, NEG_FILL)], [both[:, HD:]])


def blocks_here(shifts):
    return pltpu.VMEM((NX, len(shifts) * CAP, BLK, 2 * HD), jnp.bfloat16)


def attend_kernel(shifts, later, with_suffix, *refs):
    refs = list(refs)
    take = lambda n: [refs.pop(0) for _ in range(n)]
    me_ref, table_ref, cache_ref, z_query_ref = take(4)
    arrived = take(NX - 1)
    own_refs = take(2) if with_suffix else None
    packet_refs = take(len(shifts) + with_suffix)
    picked = take(NX - 1) if later else []
    here, query_here, packet_here = take(3)
    block_sems, query_sems, packet_sems, pick_sems = take(4)
    zo, _ = coordinates(me_ref)
    start_own_blocks(shifts, me_ref, table_ref, cache_ref, here.at[0], block_sems.at[0])
    fetches = []
    for n, shift in enumerate(shifts):
        start = pl.multiple_of(rem(zo + shift, NZ) * SUF, SUF)
        fetches.append(
            pltpu.make_async_copy(z_query_ref.at[pl.ds(start, SUF), :], query_here.at[n], query_sems.at[n])
        )
    fetches += [
        pltpu.make_async_copy(arrived[k - 1], here.at[k], block_sems.at[k]) for k in range(1, NX)
    ]
    for fetch in fetches:
        fetch.start()
    if later:
        start_picks(later, me_ref, table_ref, cache_ref, picked, pick_sems)
    sends = [
        pltpu.make_async_copy(packet_here.at[n], ref, packet_sems.at[n])
        for n, ref in enumerate(packet_refs)
    ]
    if with_suffix:
        last = len(shifts)
        part = suffix_part(head_rows(own_refs[0][...]), own_refs[1][...])
        write_packet(packet_here.at[last], *part)
        sends[last].start()
    for fetch in fetches:
        fetch.wait()
    wait_own_blocks(shifts, cache_ref, here.at[0], block_sems.at[0])
    for n, shift in enumerate(shifts):
        rows = head_rows(query_here[n])
        blocks = [here.at[k] for k in range(NX)]
        write_packet(packet_here.at[n], *cached_part(shift, n, me_ref, table_ref, rows, blocks))
        sends[n].start()
    for send in sends:
        send.wait()
    if later:
        wait_picks(later, cache_ref, picked, pick_sems)


def attend(shifts, later, me, table, cache, z_queries, arrived, own):
    keys = len(shifts) * NX * CAP * BLK
    own = list(own)
    picked = picked_shapes(later, cache.dtype) if later else []
    n_packets = len(shifts) + bool(own)
    outs = pl.pallas_call(
        functools.partial(attend_kernel, shifts, later, bool(own)),
        out_shape=[jax.ShapeDtypeStruct((PACKET, ROWS), jnp.bfloat16)] * n_packets + picked,
        in_specs=[IN_SMEM] * 2 + [IN_HBM] * (NX + 1) + [IN_VMEM] * len(own),
        out_specs=[IN_HBM] * (n_packets + len(picked)),
        scratch_shapes=[
            blocks_here(shifts),
            pltpu.VMEM((len(shifts), SUF, GROUP * HD), jnp.bfloat16),
            pltpu.VMEM((n_packets, PACKET, ROWS), jnp.bfloat16),
            pltpu.SemaphoreType.DMA((NX,)),
            pltpu.SemaphoreType.DMA((len(shifts),)),
            pltpu.SemaphoreType.DMA((n_packets,)),
            pltpu.SemaphoreType.DMA((NX - 1,)),
        ],
        compiler_params=pltpu.CompilerParams(vmem_limit_bytes=VMEM_LIMIT),
        cost_estimate=pl.CostEstimate(
            flops=4 * keys * ROWS * HD, bytes_accessed=4 * keys * HD, transcendentals=keys * ROWS
        ),
        name="attend_chunk",
    )(me, table, cache, z_queries, *arrived, *own)
    return outs[: len(shifts)], outs[len(shifts) : n_packets], outs[n_packets:]


def finish_kernel(shifts, me_ref, table_ref, cache_ref, weight_ref, query_ref, *rest):
    arrived, packet_refs = rest[: NX - 1], rest[NX - 1 : -7]
    out_ref, here, packet_here, wide, block_sems, packet_sems, wide_sem = rest[-7:]
    start_own_blocks(shifts, me_ref, table_ref, cache_ref, here.at[0], block_sems.at[0])
    fetches = [
        pltpu.make_async_copy(arrived[k - 1], here.at[k], block_sems.at[k]) for k in range(1, NX)
    ]
    packets = [
        pltpu.make_async_copy(ref, packet_here.at[n], packet_sems.at[n])
        for n, ref in enumerate(packet_refs)
    ]
    weight = pltpu.make_async_copy(weight_ref, wide, wide_sem)
    for copy in fetches + packets + [weight]:
        copy.start()
    rows = head_rows(query_ref[...])
    for fetch in fetches:
        fetch.wait()
    wait_own_blocks(shifts, cache_ref, here.at[0], block_sems.at[0])
    parts = [cached_part(0, 0, me_ref, table_ref, rows, [here.at[k] for k in range(NX)])]
    for packet in packets:
        packet.wait()
    parts += [read_packet(packet_here.at[n]) for n in range(len(packets))]
    top = functools.reduce(jnp.maximum, [part[0] for part in parts])
    factors = [jnp.exp2(part[0] - top) for part in parts]
    row_sum = sum(f * part[1] for f, part in zip(factors, parts))
    summed = sum(f * part[2] for f, part in zip(factors, parts))
    rows = (summed / row_sum).T.astype(jnp.bfloat16)
    attended = jnp.concatenate([rows[i * SUF : (i + 1) * SUF] for i in range(GROUP)], axis=1)
    weight.wait()
    out_ref[...] = jnp.dot(attended, wide[...], preferred_element_type=jnp.float32).astype(jnp.bfloat16)


def finish(shifts, me, table, cache, weight, queries, arrived, packets):
    return pl.pallas_call(
        functools.partial(finish_kernel, shifts),
        out_shape=jax.ShapeDtypeStruct((SUF, weight.shape[1]), jnp.bfloat16),
        in_specs=[IN_SMEM] * 2 + [IN_HBM] * 2 + [IN_VMEM] + [IN_HBM] * (NX - 1 + len(packets)),
        out_specs=IN_VMEM,
        scratch_shapes=[
            blocks_here(shifts),
            pltpu.VMEM((len(packets), PACKET, ROWS), jnp.bfloat16),
            pltpu.VMEM(weight.shape, weight.dtype),
            pltpu.SemaphoreType.DMA((NX,)),
            pltpu.SemaphoreType.DMA((len(packets),)),
            pltpu.SemaphoreType.DMA,
        ],
        compiler_params=pltpu.CompilerParams(vmem_limit_bytes=VMEM_LIMIT),
        cost_estimate=pl.CostEstimate(
            flops=2 * SUF * weight.size, bytes_accessed=2 * weight.size, transcendentals=0
        ),
        name="merge_project",
    )(me, table, cache, weight, queries, *arrived, *packets)


def x_permute(a, step):
    pairs = [(z * NX + x, z * NX + (x + step) % NX) for z in range(NZ) for x in range(NX)]
    return lax.ppermute(a, "store", pairs)


def z_permute(a, step):
    pairs = [(z * NX + x, ((z + step) % NZ) * NX + x) for z in range(NZ) for x in range(NX)]
    return lax.ppermute(a, "store", pairs)


def y_permute(a, step):
    pairs = [
        (y * CORES + c, ((y + step) % NY) * CORES + c) for y in range(NY) for c in range(CORES)
    ]
    return lax.ppermute(a, "head", pairs)


def core_swap(a):
    return lax.ppermute(a, "head", [(h, h ^ 1) for h in range(NY * CORES)])


def sum_heads(partial):
    core = lax.rem(lax.axis_index("head"), CORES)
    y = lax.div(lax.axis_index("head"), CORES)
    parts = partial.reshape(NY, CORES, HEAD_ROWS, partial.shape[1])
    pick_core = lambda which: lax.dynamic_index_in_dim(parts, which, 1, keepdims=False)
    other = core_swap(pick_core(1 - core))
    both = pick_core(core).astype(jnp.float32) + other.astype(jnp.float32)
    pick_y = lambda step: lax.dynamic_index_in_dim(both, rem(y + step, NY), 0, keepdims=False)
    arrived = [y_permute(pick_y(step).astype(jnp.bfloat16), step) for step in (2, 1, 3)]
    return (pick_y(0) + sum(a.astype(jnp.float32) for a in arrived)).astype(jnp.bfloat16)


def local(queries, suffix_kv, kv_cache, block_owner, block_slot, prefix_blocks, out_weight):
    store_count = lax.axis_size("store")
    me = lax.axis_index("store").astype(jnp.int32).reshape(1)
    wanted = wanted_slots(prefix_blocks, block_owner, block_slot, store_count)
    table = lax.all_to_all(wanted, "store", split_axis=0, concat_axis=0, tiled=True)
    z_groups = [[z * NX + x for z in range(NZ)] for x in range(NX)]
    z_queries = lax.all_gather(queries, "store", axis=0, tiled=True, axis_index_groups=z_groups)
    z_queries = keep_in_hbm(z_queries)
    cache = keep_in_hbm(kv_cache.reshape(kv_cache.shape[0], BLK, 2 * HD))
    suffix = suffix_kv.reshape(SUF, 2 * HD)
    picked = [pick(shifts, me, table, cache) for shifts in CHUNKS[:AHEAD]]
    packets = []
    for g, shifts in enumerate(CHUNKS[:-1]):
        arrived = [x_permute(a, k) for k, a in enumerate(picked[g], 1)]
        later = CHUNKS[g + AHEAD] if g + AHEAD < len(CHUNKS) else ()
        own = () if g else (queries, suffix)
        mine, own, more = attend(shifts, later, me, table, cache, z_queries, arrived, own)
        packets += [z_permute(packet, s) for s, packet in zip(shifts, mine)] + list(own)
        picked.append(more)
    arrived = [x_permute(a, k) for k, a in enumerate(picked[len(CHUNKS) - 1], 1)]
    return sum_heads(finish(CHUNKS[-1], me, table, cache, keep_in_hbm(out_weight), queries, arrived, packets))


def solution(mesh):
    in_specs = (
        P("store", "head"),
        P("store", "head", None),
        P("store", "head", None, None),
        P("store", None),
        P("store", None),
        P("store"),
        P("head", None),
    )
    out_specs = P(("store", "head"), None)
    return jax.shard_map(local, mesh=mesh, in_specs=in_specs, out_specs=out_specs, check_vma=False)
```

```python
import functools
import math

import jax
import jax.numpy as jnp
from jax import lax
from jax.experimental import pallas as pl
from jax.experimental.pallas import tpu as pltpu
from jax.sharding import PartitionSpec as P

HD = 128
SUF = 64
BLK = 64
CAP = 4
GROUP = 8
ROWS = SUF * GROUP
STATS = 16
PACKET = HD + STATS
NX = 4
NZ = 8
NY = 4
CORES = 2
HEAD_ROWS = SUF // (NY * CORES)

NEG_FILL = -1e30
FLOOR = -1e9
TO_LOG2 = math.log2(math.e) / math.sqrt(HD)
CHUNKS = ((4, 3, 5, 2), (6, 7, 1, 0))
WIDE_PARTS = 8
VMEM_LIMIT = 40 * 1024 * 1024

CONTRACT_LAST = (((1,), (1,)), ((), ()))
CONTRACT_FIRST = (((0,), (0,)), ((), ()))

IN_SMEM = pl.BlockSpec(memory_space=pltpu.SMEM)
IN_VMEM = pl.BlockSpec(memory_space=pltpu.VMEM)
IN_HBM = pl.BlockSpec(memory_space=pltpu.HBM)


def keep_in_hbm(a):
    return pltpu.with_memory_space_constraint(a, pltpu.HBM)


def rem(a, n):
    return lax.rem(a + n, n)


def coordinates(me_ref):
    return lax.div(me_ref[0], NX), lax.rem(me_ref[0], NX)


def wanted_kernel(length_ref, owner_ref, slot_ref, out_ref):
    count = owner_ref.shape[1]
    owners = count // CAP
    entry = lax.broadcasted_iota(jnp.int32, (1, count), 1)
    owner = jnp.where(entry < length_ref[0], owner_ref[...], owners)
    at_owner = lax.broadcasted_iota(jnp.int32, (owners, count), 0) == owner
    hits = jnp.where(at_owner, 1.0, 0.0)
    earlier = lax.broadcasted_iota(jnp.int32, (count, count), 0) < lax.broadcasted_iota(
        jnp.int32, (count, count), 1
    )
    before = jnp.dot(
        hits.astype(jnp.bfloat16),
        jnp.where(earlier, 1.0, 0.0).astype(jnp.bfloat16),
        preferred_element_type=jnp.float32,
    )
    ordinal = jnp.sum(before * hits, axis=0, keepdims=True).astype(jnp.int32)
    target = jnp.where(ordinal < CAP, owner * CAP + ordinal, count)
    chosen = jnp.where(lax.broadcasted_iota(jnp.int32, (count, count), 0) == target, 1.0, 0.0)
    slots = jnp.broadcast_to((slot_ref[...] + 1).astype(jnp.float32), (8, count))
    row = lax.dot_general(
        slots.astype(jnp.bfloat16),
        chosen.astype(jnp.bfloat16),
        CONTRACT_LAST,
        preferred_element_type=jnp.float32,
    )
    out_ref[...] = jnp.broadcast_to(
        (row[0:1].astype(jnp.int32) - 1).reshape(1, 1, count), out_ref.shape
    )


def wanted_slots(prefix_blocks, block_owner, block_slot, store_count):
    return pl.pallas_call(
        wanted_kernel,
        out_shape=jax.ShapeDtypeStruct((store_count, 1, block_owner.shape[1]), jnp.int32),
        in_specs=[IN_SMEM, IN_VMEM, IN_VMEM],
        out_specs=IN_VMEM,
        compiler_params=pltpu.CompilerParams(vmem_limit_bytes=VMEM_LIMIT),
        name="wanted_slots",
    )(prefix_blocks, block_owner, block_slot)


def slot_of(table_ref, home, owner, c, cache_ref):
    return jnp.clip(table_ref[home, 0, owner * CAP + c], 0, cache_ref.shape[0] - 1)


def start_picks(shifts, me_ref, table_ref, cache_ref, outs, sems):
    zo, xo = coordinates(me_ref)
    for k in range(NX):
        for n, shift in enumerate(shifts):
            home = rem(zo + shift, NZ) * NX + rem(xo + k, NX)
            for c in range(CAP):
                slot = slot_of(table_ref, home, me_ref[0], c, cache_ref)
                pltpu.make_async_copy(
                    cache_ref.at[pl.ds(slot, 1)],
                    outs[k].at[pl.ds(n * CAP + c, 1)],
                    sems.at[k],
                ).start()


def wait_picks(shifts, cache_ref, outs, sems):
    for k in range(NX):
        pltpu.make_async_copy(
            cache_ref.at[pl.ds(0, len(shifts) * CAP)], outs[k], sems.at[k]
        ).wait()


def picked_shapes(shifts, dtype):
    return [jax.ShapeDtypeStruct((len(shifts) * CAP, BLK, 2 * HD), dtype)] * NX


def pick_kernel(groups, me_ref, table_ref, cache_ref, *rest):
    outs, sems = rest[:-1], rest[-1]
    of_group = lambda g: outs[g * NX : (g + 1) * NX]
    for g, shifts in enumerate(groups):
        start_picks(shifts, me_ref, table_ref, cache_ref, of_group(g), sems.at[g])
    for g, shifts in enumerate(groups):
        wait_picks(shifts, cache_ref, of_group(g), sems.at[g])


def pick(groups, me, table, cache):
    shapes = [shape for shifts in groups for shape in picked_shapes(shifts, cache.dtype)]
    outs = pl.pallas_call(
        functools.partial(pick_kernel, groups),
        out_shape=shapes,
        in_specs=[IN_SMEM, IN_SMEM, IN_HBM],
        out_specs=[IN_HBM] * len(shapes),
        scratch_shapes=[pltpu.SemaphoreType.DMA((len(groups), NX))],
        compiler_params=pltpu.CompilerParams(vmem_limit_bytes=VMEM_LIMIT),
        name="pick_blocks",
    )(me, table, cache)
    return [outs[g * NX : (g + 1) * NX] for g in range(len(groups))]


def head_rows(block):
    return jnp.concatenate([block[:, i * HD : (i + 1) * HD] for i in range(GROUP)], axis=0)


def partial_sums(score_parts, value_parts):
    peak = functools.reduce(
        jnp.maximum, [jnp.max(part, axis=0, keepdims=True) for part in score_parts]
    )
    shift = jnp.maximum(peak * TO_LOG2, FLOOR).astype(jnp.bfloat16).astype(jnp.float32)
    total = jnp.zeros((1, ROWS), jnp.float32)
    acc = jnp.zeros((HD, ROWS), jnp.float32)
    for part, values in zip(score_parts, value_parts):
        expo = jnp.exp2(part * TO_LOG2 - shift)
        total += jnp.sum(expo, axis=0, keepdims=True)
        acc += lax.dot_general(
            values, expo.astype(jnp.bfloat16), CONTRACT_FIRST, preferred_element_type=jnp.float32
        )
    return shift, total, acc


def write_packet(out_ref, shift, total, acc):
    high = total.astype(jnp.bfloat16).astype(jnp.float32)
    line = lax.broadcasted_iota(jnp.int32, (STATS, ROWS), 0)
    stats = jnp.where(line == 0, shift, jnp.where(line == 1, high, jnp.where(line == 2, total - high, 0.0)))
    out_ref[:HD, :] = acc.astype(jnp.bfloat16)
    out_ref[HD:, :] = stats.astype(jnp.bfloat16)


def read_packet(ref):
    stats = ref[HD:, :].astype(jnp.float32)
    return stats[0:1], stats[1:2] + stats[2:3], ref[:HD, :].astype(jnp.float32)


def cached_part(shift, n, me_ref, table_ref, rows, blocks):
    zo, xr = coordinates(me_ref)
    home = rem(zo + shift, NZ) * NX + xr
    score_parts, value_parts = [], []
    for k in (1, 2, 3, 0):
        owner = zo * NX + rem(xr - k, NX)
        both = blocks[k][n * CAP : (n + 1) * CAP].reshape(CAP * BLK, 2 * HD)
        scores = lax.dot_general(both[:, :HD], rows, CONTRACT_LAST, preferred_element_type=jnp.float32)
        live = [
            jnp.where(
                table_ref[home, 0, owner * CAP + c] >= 0,
                scores[c * BLK : (c + 1) * BLK],
                NEG_FILL,
            )
            for c in range(CAP)
        ]
        score_parts.append(jnp.concatenate(live, axis=0))
        value_parts.append(both[:, HD:])
    return partial_sums(score_parts, value_parts)


def suffix_part(rows, both):
    scores = lax.dot_general(both[:, :HD], rows, CONTRACT_LAST, preferred_element_type=jnp.float32)
    key = lax.broadcasted_iota(jnp.int32, (SUF, ROWS), 0)
    token = lax.rem(lax.broadcasted_iota(jnp.int32, (SUF, ROWS), 1), SUF)
    return partial_sums([jnp.where(key <= token, scores, NEG_FILL)], [both[:, HD:]])


def attend_kernel(chunk, shifts, n_after, with_suffix, with_weight, *refs):
    refs = list(refs)
    take = lambda n: [refs.pop(0) for _ in range(n)]
    me_ref, table_ref, z_query_ref = take(3)
    blocks = take(NX)
    own_refs = take(2 * with_suffix)
    take(n_after)
    weight_ref = take(1)[0] if with_weight else None
    packet_refs = take(len(shifts) + with_suffix)
    wide_ref = take(1)[0] if with_weight else None
    query_here, query_sems, wide_sems = take(3)
    zo, _ = coordinates(me_ref)
    fetches = []
    for n, shift in enumerate(shifts):
        start = pl.multiple_of(rem(zo + shift, NZ) * SUF, SUF)
        fetches.append(
            pltpu.make_async_copy(z_query_ref.at[pl.ds(start, SUF), :], query_here.at[n], query_sems.at[n])
        )
        fetches[-1].start()
    wide = []
    if with_weight:
        step = weight_ref.shape[0] // WIDE_PARTS
        for n in range(WIDE_PARTS):
            part = pl.ds(n * step, step)
            wide.append(
                pltpu.make_async_copy(weight_ref.at[part, :], wide_ref.at[part, :], wide_sems.at[n])
            )
            wide[-1].start()
    if with_suffix:
        part = suffix_part(head_rows(own_refs[0][...]), own_refs[1][...])
        write_packet(packet_refs[-1], *part)
    for n, shift in enumerate(shifts):
        fetches[n].wait()
        rows = head_rows(query_here[n])
        part = cached_part(shift, chunk.index(shift), me_ref, table_ref, rows, blocks)
        write_packet(packet_refs[n], *part)
    for copy in wide:
        copy.wait()


def attend(chunk, shifts, me, table, z_queries, blocks, own=(), after=(), weight=None):
    keys = len(shifts) * NX * CAP * BLK
    with_weight = weight is not None
    n_packets = len(shifts) + bool(own)
    extra = list(after) + ([weight] if with_weight else [])
    wide = [pltpu.VMEM(weight.shape, weight.dtype)] if with_weight else []
    outs = pl.pallas_call(
        functools.partial(attend_kernel, chunk, shifts, len(after), bool(own), with_weight),
        out_shape=[jax.ShapeDtypeStruct((PACKET, ROWS), jnp.bfloat16)] * n_packets + wide,
        in_specs=[IN_SMEM] * 2 + [IN_HBM] + [IN_VMEM] * (NX + len(own)) + [IN_HBM] * len(extra),
        out_specs=[IN_VMEM] * (n_packets + len(wide)),
        scratch_shapes=[
            pltpu.VMEM((len(shifts), SUF, GROUP * HD), jnp.bfloat16),
            pltpu.SemaphoreType.DMA((len(shifts),)),
            pltpu.SemaphoreType.DMA((WIDE_PARTS,)),
        ],
        compiler_params=pltpu.CompilerParams(vmem_limit_bytes=VMEM_LIMIT),
        cost_estimate=pl.CostEstimate(
            flops=4 * keys * ROWS * HD, bytes_accessed=4 * keys * HD, transcendentals=keys * ROWS
        ),
        name="attend_chunk",
    )(me, table, z_queries, *blocks, *own, *extra)
    return outs[:n_packets], outs[n_packets:]


def finish_kernel(wide_ref, *rest):
    packet_refs, out_ref = rest[:-1], rest[-1]
    parts = [read_packet(ref) for ref in packet_refs]
    top = functools.reduce(jnp.maximum, [part[0] for part in parts])
    factors = [jnp.exp2(part[0] - top) for part in parts]
    row_sum = sum(f * part[1] for f, part in zip(factors, parts))
    summed = sum(f * part[2] for f, part in zip(factors, parts))
    rows = (summed / row_sum).T.astype(jnp.bfloat16)
    attended = jnp.concatenate([rows[i * SUF : (i + 1) * SUF] for i in range(GROUP)], axis=1)
    out_ref[...] = jnp.dot(
        attended, wide_ref[...], preferred_element_type=jnp.float32
    ).astype(jnp.bfloat16)


def finish(wide, packets):
    return pl.pallas_call(
        finish_kernel,
        out_shape=jax.ShapeDtypeStruct((SUF, wide.shape[1]), jnp.bfloat16),
        compiler_params=pltpu.CompilerParams(vmem_limit_bytes=VMEM_LIMIT),
        cost_estimate=pl.CostEstimate(
            flops=2 * SUF * wide.size, bytes_accessed=2 * wide.size, transcendentals=0
        ),
        name="merge_project",
    )(wide, *packets)


def x_permute(a, step):
    pairs = [(z * NX + x, z * NX + (x + step) % NX) for z in range(NZ) for x in range(NX)]
    return lax.ppermute(a, "store", pairs)


def z_permute(a, step):
    pairs = [(z * NX + x, ((z + step) % NZ) * NX + x) for z in range(NZ) for x in range(NX)]
    return lax.ppermute(a, "store", pairs)


def y_permute(a, step):
    pairs = [
        (y * CORES + c, ((y + step) % NY) * CORES + c) for y in range(NY) for c in range(CORES)
    ]
    return lax.ppermute(a, "head", pairs)


def core_swap(a):
    return lax.ppermute(a, "head", [(h, h ^ 1) for h in range(NY * CORES)])


def sum_heads(partial):
    core = lax.rem(lax.axis_index("head"), CORES)
    y = lax.div(lax.axis_index("head"), CORES)
    parts = partial.reshape(NY, CORES, HEAD_ROWS, partial.shape[1])
    pick_core = lambda which: lax.dynamic_index_in_dim(parts, which, 1, keepdims=False)
    other = core_swap(pick_core(1 - core))
    both = pick_core(core).astype(jnp.float32) + other.astype(jnp.float32)
    pick_y = lambda step: lax.dynamic_index_in_dim(both, rem(y + step, NY), 0, keepdims=False)
    arrived = [y_permute(pick_y(step).astype(jnp.bfloat16), step) for step in (2, 1, 3)]
    return (pick_y(0) + sum(a.astype(jnp.float32) for a in arrived)).astype(jnp.bfloat16)


def local(queries, suffix_kv, kv_cache, block_owner, block_slot, prefix_blocks, out_weight):
    store_count = lax.axis_size("store")
    me = lax.axis_index("store").astype(jnp.int32).reshape(1)
    wanted = wanted_slots(prefix_blocks, block_owner, block_slot, store_count)
    table = lax.all_to_all(wanted, "store", split_axis=0, concat_axis=0, tiled=True)
    z_groups = [[z * NX + x for z in range(NZ)] for x in range(NX)]
    z_queries = lax.all_gather(queries, "store", axis=0, tiled=True, axis_index_groups=z_groups)
    z_queries = keep_in_hbm(z_queries)
    cache = keep_in_hbm(kv_cache.reshape(kv_cache.shape[0], BLK, 2 * HD))
    suffix = suffix_kv.reshape(SUF, 2 * HD)
    far, near = CHUNKS
    away = near[:-1]
    far_picked, near_picked = pick(CHUNKS, me, table, cache)
    over_x = lambda blocks: [blocks[0]] + [x_permute(blocks[k], k) for k in range(1, NX)]
    over_z = lambda shifts, parts: [z_permute(part, s) for s, part in zip(shifts, parts)]
    far_blocks, near_blocks = over_x(far_picked), over_x(near_picked)
    parts, _ = attend(far, far, me, table, z_queries, far_blocks, own=(queries, suffix))
    packets = over_z(far, parts) + [parts[-1]]
    parts, _ = attend(near, away, me, table, z_queries, near_blocks, after=packets[:2])
    packets += over_z(away, parts)
    home, (wide,) = attend(
        near, near[-1:], me, table, z_queries, near_blocks, after=parts[:1], weight=keep_in_hbm(out_weight)
    )
    return sum_heads(finish(wide, packets + list(home)))


def solution(mesh):
    in_specs = (
        P("store", "head"),
        P("store", "head", None),
        P("store", "head", None, None),
        P("store", None),
        P("store", None),
        P("store"),
        P("head", None),
    )
    out_specs = P(("store", "head"), None)
    return jax.shard_map(local, mesh=mesh, in_specs=in_specs, out_specs=out_specs, check_vma=False)
```

```python
import functools
import math

import jax
import jax.numpy as jnp
from jax import lax
from jax.experimental import pallas as pl
from jax.experimental.pallas import tpu as pltpu
from jax.sharding import PartitionSpec as P

HD = 128
SUF = 64
BLK = 64
CAP = 4
GROUP = 8
ROWS = SUF * GROUP
STATS = 16
PACKET = HD + STATS
NX = 4
NZ = 8
NY = 4
CORES = 2
HEAD_ROWS = SUF // (NY * CORES)

NEG_FILL = -1e30
FLOOR = -1e9
TO_LOG2 = math.log2(math.e) / math.sqrt(HD)
CHUNKS = ((4, 3, 5, 2), (6, 7, 1, 0))
WIDE_PARTS = 8
VMEM_LIMIT = 24 * 1024 * 1024

CONTRACT_LAST = (((1,), (1,)), ((), ()))
CONTRACT_FIRST = (((0,), (0,)), ((), ()))

IN_SMEM = pl.BlockSpec(memory_space=pltpu.SMEM)
IN_VMEM = pl.BlockSpec(memory_space=pltpu.VMEM)
IN_HBM = pl.BlockSpec(memory_space=pltpu.HBM)


def keep_in_hbm(a):
    return pltpu.with_memory_space_constraint(a, pltpu.HBM)


def rem(a, n):
    return lax.rem(a + n, n)


def coordinates(me_ref):
    return lax.div(me_ref[0], NX), lax.rem(me_ref[0], NX)


def wanted_kernel(length_ref, owner_ref, slot_ref, out_ref):
    count = owner_ref.shape[1]
    owners = count // CAP
    entry = lax.broadcasted_iota(jnp.int32, (1, count), 1)
    owner = jnp.where(entry < length_ref[0], owner_ref[...], owners)
    at_owner = lax.broadcasted_iota(jnp.int32, (owners, count), 0) == owner
    hits = jnp.where(at_owner, 1.0, 0.0)
    earlier = lax.broadcasted_iota(jnp.int32, (count, count), 0) < lax.broadcasted_iota(
        jnp.int32, (count, count), 1
    )
    before = jnp.dot(
        hits.astype(jnp.bfloat16),
        jnp.where(earlier, 1.0, 0.0).astype(jnp.bfloat16),
        preferred_element_type=jnp.float32,
    )
    ordinal = jnp.sum(before * hits, axis=0, keepdims=True).astype(jnp.int32)
    target = jnp.where(ordinal < CAP, owner * CAP + ordinal, count)
    chosen = jnp.where(lax.broadcasted_iota(jnp.int32, (count, count), 0) == target, 1.0, 0.0)
    slots = jnp.broadcast_to((slot_ref[...] + 1).astype(jnp.float32), (8, count))
    row = lax.dot_general(
        slots.astype(jnp.bfloat16),
        chosen.astype(jnp.bfloat16),
        CONTRACT_LAST,
        preferred_element_type=jnp.float32,
    )
    out_ref[...] = jnp.broadcast_to(
        (row[0:1].astype(jnp.int32) - 1).reshape(1, 1, count), out_ref.shape
    )


def wanted_slots(prefix_blocks, block_owner, block_slot, store_count):
    return pl.pallas_call(
        wanted_kernel,
        out_shape=jax.ShapeDtypeStruct((store_count, 1, block_owner.shape[1]), jnp.int32),
        in_specs=[IN_SMEM, IN_VMEM, IN_VMEM],
        out_specs=IN_VMEM,
        compiler_params=pltpu.CompilerParams(vmem_limit_bytes=VMEM_LIMIT),
        name="wanted_slots",
    )(prefix_blocks, block_owner, block_slot)


def slot_of(table_ref, home, owner, c, cache_ref):
    return jnp.clip(table_ref[home, 0, owner * CAP + c], 0, cache_ref.shape[0] - 1)


def pick_kernel(wanted, me_ref, table_ref, cache_ref, *rest):
    outs, sems = rest[:-1], rest[-1]
    zo, xo = coordinates(me_ref)
    for m, (shifts, k) in enumerate(wanted):
        for n, shift in enumerate(shifts):
            home = rem(zo + shift, NZ) * NX + rem(xo + k, NX)
            for c in range(CAP):
                slot = slot_of(table_ref, home, me_ref[0], c, cache_ref)
                pltpu.make_async_copy(
                    cache_ref.at[pl.ds(slot, 1)],
                    outs[m].at[pl.ds(n * CAP + c, 1)],
                    sems.at[m],
                ).start()
    for m, (shifts, k) in enumerate(wanted):
        pltpu.make_async_copy(
            cache_ref.at[pl.ds(0, len(shifts) * CAP)], outs[m], sems.at[m]
        ).wait()


def pick(wanted, me, table, cache):
    return pl.pallas_call(
        functools.partial(pick_kernel, wanted),
        out_shape=[
            pltpu.VMEM((len(shifts) * CAP, BLK, 2 * HD), cache.dtype) for shifts, k in wanted
        ],
        in_specs=[IN_SMEM, IN_SMEM, IN_HBM],
        out_specs=[IN_VMEM] * len(wanted),
        scratch_shapes=[pltpu.SemaphoreType.DMA((len(wanted),))],
        compiler_params=pltpu.CompilerParams(vmem_limit_bytes=VMEM_LIMIT),
        name="pick_blocks",
    )(me, table, cache)


def head_rows(block):
    return jnp.concatenate([block[:, i * HD : (i + 1) * HD] for i in range(GROUP)], axis=0)


def partial_sums(score_parts, value_parts):
    peak = functools.reduce(
        jnp.maximum, [jnp.max(part, axis=0, keepdims=True) for part in score_parts]
    )
    shift = jnp.maximum(peak * TO_LOG2, FLOOR).astype(jnp.bfloat16).astype(jnp.float32)
    total = jnp.zeros((1, ROWS), jnp.float32)
    acc = jnp.zeros((HD, ROWS), jnp.float32)
    for part, values in zip(score_parts, value_parts):
        expo = jnp.exp2(part * TO_LOG2 - shift)
        total += jnp.sum(expo, axis=0, keepdims=True)
        acc += lax.dot_general(
            values, expo.astype(jnp.bfloat16), CONTRACT_FIRST, preferred_element_type=jnp.float32
        )
    return shift, total, acc


def write_packet(out_ref, shift, total, acc):
    high = total.astype(jnp.bfloat16).astype(jnp.float32)
    line = lax.broadcasted_iota(jnp.int32, (STATS, ROWS), 0)
    stats = jnp.where(line == 0, shift, jnp.where(line == 1, high, jnp.where(line == 2, total - high, 0.0)))
    out_ref[:HD, :] = acc.astype(jnp.bfloat16)
    out_ref[HD:, :] = stats.astype(jnp.bfloat16)


def read_packet(ref):
    stats = ref[HD:, :].astype(jnp.float32)
    return stats[0:1], stats[1:2] + stats[2:3], ref[:HD, :].astype(jnp.float32)


def cached_part(shift, n, me_ref, table_ref, rows, blocks):
    zo, xr = coordinates(me_ref)
    home = rem(zo + shift, NZ) * NX + xr
    score_parts, value_parts = [], []
    for k in (1, 2, 3, 0):
        owner = zo * NX + rem(xr - k, NX)
        both = blocks[k][n * CAP : (n + 1) * CAP].reshape(CAP * BLK, 2 * HD)
        scores = lax.dot_general(both[:, :HD], rows, CONTRACT_LAST, preferred_element_type=jnp.float32)
        live = [
            jnp.where(
                table_ref[home, 0, owner * CAP + c] >= 0,
                scores[c * BLK : (c + 1) * BLK],
                NEG_FILL,
            )
            for c in range(CAP)
        ]
        score_parts.append(jnp.concatenate(live, axis=0))
        value_parts.append(both[:, HD:])
    return partial_sums(score_parts, value_parts)


def suffix_part(rows, both):
    scores = lax.dot_general(both[:, :HD], rows, CONTRACT_LAST, preferred_element_type=jnp.float32)
    key = lax.broadcasted_iota(jnp.int32, (SUF, ROWS), 0)
    token = lax.rem(lax.broadcasted_iota(jnp.int32, (SUF, ROWS), 1), SUF)
    return partial_sums([jnp.where(key <= token, scores, NEG_FILL)], [both[:, HD:]])


def attend_kernel(chunk, shifts, n_after, with_suffix, with_weight, *refs):
    refs = list(refs)
    take = lambda n: [refs.pop(0) for _ in range(n)]
    me_ref, table_ref, z_query_ref = take(3)
    blocks = take(NX)
    own_refs = take(2 * with_suffix)
    take(n_after)
    weight_ref = take(1)[0] if with_weight else None
    packet_refs = take(len(shifts) + with_suffix)
    wide_ref = take(1)[0] if with_weight else None
    query_here, query_sems, wide_sems = take(3)
    zo, _ = coordinates(me_ref)
    fetches = []
    for n, shift in enumerate(shifts):
        start = pl.multiple_of(rem(zo + shift, NZ) * SUF, SUF)
        fetches.append(
            pltpu.make_async_copy(z_query_ref.at[pl.ds(start, SUF), :], query_here.at[n], query_sems.at[n])
        )
        fetches[-1].start()
    wide = []
    if with_weight:
        step = weight_ref.shape[0] // WIDE_PARTS
        for n in range(WIDE_PARTS):
            part = pl.ds(n * step, step)
            wide.append(
                pltpu.make_async_copy(weight_ref.at[part, :], wide_ref.at[part, :], wide_sems.at[n])
            )
            wide[-1].start()
    if with_suffix:
        part = suffix_part(head_rows(own_refs[0][...]), own_refs[1][...])
        write_packet(packet_refs[-1], *part)
    for n, shift in enumerate(shifts):
        fetches[n].wait()
        rows = head_rows(query_here[n])
        part = cached_part(shift, chunk.index(shift), me_ref, table_ref, rows, blocks)
        write_packet(packet_refs[n], *part)
    for copy in wide:
        copy.wait()


def attend(chunk, shifts, me, table, z_queries, blocks, own=(), after=(), weight=None):
    keys = len(shifts) * NX * CAP * BLK
    with_weight = weight is not None
    n_packets = len(shifts) + bool(own)
    extra = list(after) + ([weight] if with_weight else [])
    wide = [pltpu.VMEM(weight.shape, weight.dtype)] if with_weight else []
    outs = pl.pallas_call(
        functools.partial(attend_kernel, chunk, shifts, len(after), bool(own), with_weight),
        out_shape=[jax.ShapeDtypeStruct((PACKET, ROWS), jnp.bfloat16)] * n_packets + wide,
        in_specs=[IN_SMEM] * 2 + [IN_HBM] + [IN_VMEM] * (NX + len(own)) + [IN_HBM] * len(extra),
        out_specs=[IN_VMEM] * (n_packets + len(wide)),
        scratch_shapes=[
            pltpu.VMEM((len(shifts), SUF, GROUP * HD), jnp.bfloat16),
            pltpu.SemaphoreType.DMA((len(shifts),)),
            pltpu.SemaphoreType.DMA((WIDE_PARTS,)),
        ],
        compiler_params=pltpu.CompilerParams(vmem_limit_bytes=VMEM_LIMIT),
        cost_estimate=pl.CostEstimate(
            flops=4 * keys * ROWS * HD, bytes_accessed=4 * keys * HD, transcendentals=keys * ROWS
        ),
        name="attend_chunk",
    )(me, table, z_queries, *blocks, *own, *extra)
    return outs[:n_packets], outs[n_packets:]


def finish_kernel(wide_ref, *rest):
    packet_refs, out_ref = rest[:-1], rest[-1]
    parts = [read_packet(ref) for ref in packet_refs]
    top = functools.reduce(jnp.maximum, [part[0] for part in parts])
    factors = [jnp.exp2(part[0] - top) for part in parts]
    row_sum = sum(f * part[1] for f, part in zip(factors, parts))
    summed = sum(f * part[2] for f, part in zip(factors, parts))
    rows = (summed / row_sum).T.astype(jnp.bfloat16)
    attended = jnp.concatenate([rows[i * SUF : (i + 1) * SUF] for i in range(GROUP)], axis=1)
    out_ref[...] = jnp.dot(
        attended, wide_ref[...], preferred_element_type=jnp.float32
    ).astype(jnp.bfloat16)


def finish(wide, packets):
    return pl.pallas_call(
        finish_kernel,
        out_shape=jax.ShapeDtypeStruct((SUF, wide.shape[1]), jnp.bfloat16),
        compiler_params=pltpu.CompilerParams(vmem_limit_bytes=VMEM_LIMIT),
        cost_estimate=pl.CostEstimate(
            flops=2 * SUF * wide.size, bytes_accessed=2 * wide.size, transcendentals=0
        ),
        name="merge_project",
    )(wide, *packets)


def x_permute(a, step):
    pairs = [(z * NX + x, z * NX + (x + step) % NX) for z in range(NZ) for x in range(NX)]
    return lax.ppermute(a, "store", pairs)


def z_permute(a, step):
    pairs = [(z * NX + x, ((z + step) % NZ) * NX + x) for z in range(NZ) for x in range(NX)]
    return lax.ppermute(a, "store", pairs)


def y_permute(a, step):
    pairs = [
        (y * CORES + c, ((y + step) % NY) * CORES + c) for y in range(NY) for c in range(CORES)
    ]
    return lax.ppermute(a, "head", pairs)


def core_swap(a):
    return lax.ppermute(a, "head", [(h, h ^ 1) for h in range(NY * CORES)])


def sum_heads(partial):
    core = lax.rem(lax.axis_index("head"), CORES)
    y = lax.div(lax.axis_index("head"), CORES)
    parts = partial.reshape(NY, CORES, HEAD_ROWS, partial.shape[1])
    pick_core = lambda which: lax.dynamic_index_in_dim(parts, which, 1, keepdims=False)
    other = core_swap(pick_core(1 - core))
    both = pick_core(core).astype(jnp.float32) + other.astype(jnp.float32)
    pick_y = lambda step: lax.dynamic_index_in_dim(both, rem(y + step, NY), 0, keepdims=False)
    arrived = [y_permute(pick_y(step).astype(jnp.bfloat16), step) for step in (2, 1, 3)]
    return (pick_y(0) + sum(a.astype(jnp.float32) for a in arrived)).astype(jnp.bfloat16)


def local(queries, suffix_kv, kv_cache, block_owner, block_slot, prefix_blocks, out_weight):
    store_count = lax.axis_size("store")
    me = lax.axis_index("store").astype(jnp.int32).reshape(1)
    wanted = wanted_slots(prefix_blocks, block_owner, block_slot, store_count)
    table = lax.all_to_all(wanted, "store", split_axis=0, concat_axis=0, tiled=True)
    z_groups = [[z * NX + x for z in range(NZ)] for x in range(NX)]
    z_queries = lax.all_gather(queries, "store", axis=0, tiled=True, axis_index_groups=z_groups)
    z_queries = keep_in_hbm(z_queries)
    cache = keep_in_hbm(kv_cache.reshape(kv_cache.shape[0], BLK, 2 * HD))
    suffix = suffix_kv.reshape(SUF, 2 * HD)
    far, near = CHUNKS
    away = near[:-1]
    steps = range(1, NX)
    far_sent = pick([(far, k) for k in steps], me, table, cache)
    *near_sent, far_here, near_here = pick(
        [(near, k) for k in steps] + [(far, 0), (near, 0)], me, table, cache
    )
    over_x = lambda blocks: [x_permute(block, k) for k, block in zip(steps, blocks)]
    over_z = lambda shifts, parts: [z_permute(part, s) for s, part in zip(shifts, parts)]
    far_blocks, near_blocks = [far_here] + over_x(far_sent), [near_here] + over_x(near_sent)
    parts, _ = attend(far, far, me, table, z_queries, far_blocks, own=(queries, suffix))
    packets = over_z(far, parts) + [parts[-1]]
    parts, _ = attend(near, away, me, table, z_queries, near_blocks, after=packets[:1])
    packets += over_z(away, parts)
    home, (wide,) = attend(
        near, near[-1:], me, table, z_queries, near_blocks, after=parts[:1], weight=keep_in_hbm(out_weight)
    )
    return sum_heads(finish(wide, packets + list(home)))


def solution(mesh):
    in_specs = (
        P("store", "head"),
        P("store", "head", None),
        P("store", "head", None, None),
        P("store", None),
        P("store", None),
        P("store"),
        P("head", None),
    )
    out_specs = P(("store", "head"), None)
    return jax.shard_map(local, mesh=mesh, in_specs=in_specs, out_specs=out_specs, check_vma=False)
```

```python
import functools
import math

import jax
import jax.numpy as jnp
from jax import lax
from jax.experimental import pallas as pl
from jax.experimental.pallas import tpu as pltpu
from jax.sharding import PartitionSpec as P

HD = 128
SUF = 64
BLK = 64
CAP = 4
GROUP = 8
ROWS = SUF * GROUP
STATS = 16
PACKET = HD + STATS
NX = 4
NZ = 8
NY = 4
CORES = 2
HEAD_ROWS = SUF // (NY * CORES)

NEG_FILL = -1e30
FLOOR = -1e9
TO_LOG2 = math.log2(math.e) / math.sqrt(HD)
CHUNKS = ((4, 3, 5, 2), (6, 7, 1, 0))
WIDE_PARTS = 8
VMEM_LIMIT = 24 * 1024 * 1024

CONTRACT_LAST = (((1,), (1,)), ((), ()))
CONTRACT_FIRST = (((0,), (0,)), ((), ()))

IN_SMEM = pl.BlockSpec(memory_space=pltpu.SMEM)
IN_VMEM = pl.BlockSpec(memory_space=pltpu.VMEM)
IN_HBM = pl.BlockSpec(memory_space=pltpu.HBM)


def keep_in_hbm(a):
    return pltpu.with_memory_space_constraint(a, pltpu.HBM)


def rem(a, n):
    return lax.rem(a + n, n)


def coordinates(me_ref):
    return lax.div(me_ref[0], NX), lax.rem(me_ref[0], NX)


def wanted_kernel(length_ref, owner_ref, slot_ref, out_ref):
    count = owner_ref.shape[1]
    owners = count // CAP
    entry = lax.broadcasted_iota(jnp.int32, (1, count), 1)
    owner = jnp.where(entry < length_ref[0], owner_ref[...], owners)
    at_owner = lax.broadcasted_iota(jnp.int32, (owners, count), 0) == owner
    hits = jnp.where(at_owner, 1.0, 0.0)
    earlier = lax.broadcasted_iota(jnp.int32, (count, count), 0) < lax.broadcasted_iota(
        jnp.int32, (count, count), 1
    )
    before = jnp.dot(
        hits.astype(jnp.bfloat16),
        jnp.where(earlier, 1.0, 0.0).astype(jnp.bfloat16),
        preferred_element_type=jnp.float32,
    )
    ordinal = jnp.sum(before * hits, axis=0, keepdims=True).astype(jnp.int32)
    target = jnp.where(ordinal < CAP, owner * CAP + ordinal, count)
    chosen = jnp.where(lax.broadcasted_iota(jnp.int32, (count, count), 0) == target, 1.0, 0.0)
    slots = jnp.broadcast_to((slot_ref[...] + 1).astype(jnp.float32), (8, count))
    row = lax.dot_general(
        slots.astype(jnp.bfloat16),
        chosen.astype(jnp.bfloat16),
        CONTRACT_LAST,
        preferred_element_type=jnp.float32,
    )
    out_ref[...] = jnp.broadcast_to(
        (row[0:1].astype(jnp.int32) - 1).reshape(1, 1, count), out_ref.shape
    )


def wanted_slots(prefix_blocks, block_owner, block_slot, store_count):
    return pl.pallas_call(
        wanted_kernel,
        out_shape=jax.ShapeDtypeStruct((store_count, 1, block_owner.shape[1]), jnp.int32),
        in_specs=[IN_SMEM, IN_VMEM, IN_VMEM],
        out_specs=IN_VMEM,
        compiler_params=pltpu.CompilerParams(vmem_limit_bytes=VMEM_LIMIT),
        name="wanted_slots",
    )(prefix_blocks, block_owner, block_slot)


def slot_of(table_ref, home, owner, c, cache_ref):
    return jnp.clip(table_ref[home, 0, owner * CAP + c], 0, cache_ref.shape[0] - 1)


def start_picks(shifts, k, me_ref, table_ref, cache_ref, out, sem):
    zo, xo = coordinates(me_ref)
    for n, shift in enumerate(shifts):
        home = rem(zo + shift, NZ) * NX + rem(xo + k, NX)
        for c in range(CAP):
            slot = slot_of(table_ref, home, me_ref[0], c, cache_ref)
            pltpu.make_async_copy(
                cache_ref.at[pl.ds(slot, 1)], out.at[pl.ds(n * CAP + c, 1)], sem
            ).start()


def wait_picks(shifts, cache_ref, out, sem):
    pltpu.make_async_copy(cache_ref.at[pl.ds(0, len(shifts) * CAP)], out, sem).wait()


def pick_far_kernel(shifts, me_ref, table_ref, cache_ref, query_ref, *refs):
    outs, (copies_ref, query_here, sems, query_sem, copy_sems) = refs[: NX - 1], refs[NX - 1 :]
    fetch = pltpu.make_async_copy(query_ref, query_here, query_sem)
    fetch.start()
    for k, out in enumerate(outs, 1):
        start_picks(shifts, k, me_ref, table_ref, cache_ref, out, sems.at[k - 1])
    copies = [
        pltpu.make_async_copy(query_here, copies_ref.at[z], copy_sems.at[z]) for z in range(NZ)
    ]
    fetch.wait()
    for copy in copies:
        copy.start()
    for k, out in enumerate(outs, 1):
        wait_picks(shifts, cache_ref, out, sems.at[k - 1])
    for copy in copies:
        copy.wait()


def pick_far(shifts, me, table, cache, queries):
    block = (len(shifts) * CAP, BLK, 2 * HD)
    *sent, copies = pl.pallas_call(
        functools.partial(pick_far_kernel, shifts),
        out_shape=[pltpu.VMEM(block, cache.dtype)] * (NX - 1)
        + [jax.ShapeDtypeStruct((NZ,) + queries.shape, queries.dtype)],
        in_specs=[IN_SMEM, IN_SMEM, IN_HBM, IN_HBM],
        out_specs=[IN_VMEM] * (NX - 1) + [IN_HBM],
        scratch_shapes=[
            pltpu.VMEM(queries.shape, queries.dtype),
            pltpu.SemaphoreType.DMA((NX - 1,)),
            pltpu.SemaphoreType.DMA,
            pltpu.SemaphoreType.DMA((NZ,)),
        ],
        compiler_params=pltpu.CompilerParams(vmem_limit_bytes=VMEM_LIMIT),
        name="pick_far",
    )(me, table, cache, keep_in_hbm(queries))
    return sent, copies


def pick_near_kernel(shifts, me_ref, table_ref, cache_ref, *refs):
    outs, here, sems = refs[: NX - 1], refs[-2], refs[-1]
    for k in range(1, NX):
        start_picks(shifts, k, me_ref, table_ref, cache_ref, here.at[k - 1], sems.at[k - 1])
    moves = []
    for k, out in enumerate(outs, 1):
        wait_picks(shifts, cache_ref, here.at[k - 1], sems.at[k - 1])
        moves.append(pltpu.make_async_copy(here.at[k - 1], out, sems.at[k - 1]))
        moves[-1].start()
    for move in moves:
        move.wait()


def pick_near(shifts, me, table, cache):
    block = (len(shifts) * CAP, BLK, 2 * HD)
    return pl.pallas_call(
        functools.partial(pick_near_kernel, shifts),
        out_shape=[jax.ShapeDtypeStruct(block, cache.dtype)] * (NX - 1),
        in_specs=[IN_SMEM, IN_SMEM, IN_HBM],
        out_specs=[IN_HBM] * (NX - 1),
        scratch_shapes=[
            pltpu.VMEM((NX - 1,) + block, cache.dtype),
            pltpu.SemaphoreType.DMA((NX - 1,)),
        ],
        compiler_params=pltpu.CompilerParams(vmem_limit_bytes=VMEM_LIMIT),
        name="pick_near",
    )(me, table, cache)


def head_rows(block):
    return jnp.concatenate([block[:, i * HD : (i + 1) * HD] for i in range(GROUP)], axis=0)


def partial_sums(score_parts, value_parts):
    peak = functools.reduce(
        jnp.maximum, [jnp.max(part, axis=0, keepdims=True) for part in score_parts]
    )
    shift = jnp.maximum(peak * TO_LOG2, FLOOR).astype(jnp.bfloat16).astype(jnp.float32)
    total = jnp.zeros((1, ROWS), jnp.float32)
    acc = jnp.zeros((HD, ROWS), jnp.float32)
    for part, values in zip(score_parts, value_parts):
        expo = jnp.exp2(part * TO_LOG2 - shift)
        total += jnp.sum(expo, axis=0, keepdims=True)
        acc += lax.dot_general(
            values, expo.astype(jnp.bfloat16), CONTRACT_FIRST, preferred_element_type=jnp.float32
        )
    return shift, total, acc


def write_packet(out_ref, shift, total, acc):
    high = total.astype(jnp.bfloat16).astype(jnp.float32)
    line = lax.broadcasted_iota(jnp.int32, (STATS, ROWS), 0)
    stats = jnp.where(line == 0, shift, jnp.where(line == 1, high, jnp.where(line == 2, total - high, 0.0)))
    out_ref[:HD, :] = acc.astype(jnp.bfloat16)
    out_ref[HD:, :] = stats.astype(jnp.bfloat16)


def read_packet(ref):
    stats = ref[HD:, :].astype(jnp.float32)
    return stats[0:1], stats[1:2] + stats[2:3], ref[:HD, :].astype(jnp.float32)


def cached_part(shift, n, me_ref, table_ref, rows, blocks):
    zo, xr = coordinates(me_ref)
    home = rem(zo + shift, NZ) * NX + xr
    score_parts, value_parts = [], []
    for k in (1, 2, 3, 0):
        owner = zo * NX + rem(xr - k, NX)
        both = blocks[k][n * CAP : (n + 1) * CAP].reshape(CAP * BLK, 2 * HD)
        scores = lax.dot_general(both[:, :HD], rows, CONTRACT_LAST, preferred_element_type=jnp.float32)
        live = [
            jnp.where(
                table_ref[home, 0, owner * CAP + c] >= 0,
                scores[c * BLK : (c + 1) * BLK],
                NEG_FILL,
            )
            for c in range(CAP)
        ]
        score_parts.append(jnp.concatenate(live, axis=0))
        value_parts.append(both[:, HD:])
    return partial_sums(score_parts, value_parts)


def suffix_part(rows, both):
    scores = lax.dot_general(both[:, :HD], rows, CONTRACT_LAST, preferred_element_type=jnp.float32)
    key = lax.broadcasted_iota(jnp.int32, (SUF, ROWS), 0)
    token = lax.rem(lax.broadcasted_iota(jnp.int32, (SUF, ROWS), 1), SUF)
    return partial_sums([jnp.where(key <= token, scores, NEG_FILL)], [both[:, HD:]])


def attend_kernel(chunk, shifts, n_after, with_suffix, with_weight, *refs):
    refs = list(refs)
    take = lambda n: [refs.pop(0) for _ in range(n)]
    me_ref, table_ref, cache_ref, z_query_ref = take(4)
    arrived = take(NX - 1)
    own_refs = take(2 * with_suffix)
    take(n_after)
    weight_ref = take(1)[0] if with_weight else None
    packet_refs = take(len(shifts) + with_suffix)
    wide_ref = take(1)[0] if with_weight else None
    here, query_here, block_sems, query_sems, wide_sems = take(5)
    zo, _ = coordinates(me_ref)
    first = chunk.index(shifts[0]) * CAP
    fetches = [
        pltpu.make_async_copy(
            arrived[k - 1].at[pl.ds(first, len(shifts) * CAP)], here.at[k], block_sems.at[k]
        )
        for k in range(1, NX)
    ]
    for n, shift in enumerate(shifts):
        fetches.append(
            pltpu.make_async_copy(
                z_query_ref.at[rem(zo + shift, NZ)], query_here.at[n], query_sems.at[n]
            )
        )
    for fetch in fetches:
        fetch.start()
    start_picks(shifts, 0, me_ref, table_ref, cache_ref, here.at[0], block_sems.at[0])
    wide = []
    if with_weight:
        step = weight_ref.shape[0] // WIDE_PARTS
        for n in range(WIDE_PARTS):
            part = pl.ds(n * step, step)
            wide.append(
                pltpu.make_async_copy(weight_ref.at[part, :], wide_ref.at[part, :], wide_sems.at[n])
            )
            wide[-1].start()
    if with_suffix:
        part = suffix_part(head_rows(own_refs[0][...]), own_refs[1][...])
        write_packet(packet_refs[-1], *part)
    for fetch in fetches:
        fetch.wait()
    wait_picks(shifts, cache_ref, here.at[0], block_sems.at[0])
    for n, shift in enumerate(shifts):
        rows = head_rows(query_here[n])
        part = cached_part(shift, n, me_ref, table_ref, rows, [here.at[k] for k in range(NX)])
        write_packet(packet_refs[n], *part)
    for copy in wide:
        copy.wait()


def attend(chunk, shifts, me, table, cache, z_queries, arrived, own=(), after=(), weight=None):
    keys = len(shifts) * NX * CAP * BLK
    with_weight = weight is not None
    n_packets = len(shifts) + bool(own)
    extra = list(after) + ([weight] if with_weight else [])
    wide = [pltpu.VMEM(weight.shape, weight.dtype)] if with_weight else []
    outs = pl.pallas_call(
        functools.partial(attend_kernel, chunk, shifts, len(after), bool(own), with_weight),
        out_shape=[jax.ShapeDtypeStruct((PACKET, ROWS), jnp.bfloat16)] * n_packets + wide,
        in_specs=[IN_SMEM] * 2 + [IN_HBM] * (NX + 1) + [IN_VMEM] * len(own) + [IN_HBM] * len(extra),
        out_specs=[IN_VMEM] * (n_packets + len(wide)),
        scratch_shapes=[
            pltpu.VMEM((NX, len(shifts) * CAP, BLK, 2 * HD), cache.dtype),
            pltpu.VMEM((len(shifts), SUF, GROUP * HD), jnp.bfloat16),
            pltpu.SemaphoreType.DMA((NX,)),
            pltpu.SemaphoreType.DMA((len(shifts),)),
            pltpu.SemaphoreType.DMA((WIDE_PARTS,)),
        ],
        compiler_params=pltpu.CompilerParams(vmem_limit_bytes=VMEM_LIMIT),
        cost_estimate=pl.CostEstimate(
            flops=4 * keys * ROWS * HD, bytes_accessed=4 * keys * HD, transcendentals=keys * ROWS
        ),
        name="attend_chunk",
    )(me, table, cache, z_queries, *arrived, *own, *extra)
    return outs[:n_packets], outs[n_packets:]


def finish_kernel(wide_ref, *rest):
    packet_refs, out_ref = rest[:-1], rest[-1]
    parts = [read_packet(ref) for ref in packet_refs]
    top = functools.reduce(jnp.maximum, [part[0] for part in parts])
    factors = [jnp.exp2(part[0] - top) for part in parts]
    row_sum = sum(f * part[1] for f, part in zip(factors, parts))
    summed = sum(f * part[2] for f, part in zip(factors, parts))
    rows = (summed / row_sum).T.astype(jnp.bfloat16)
    attended = jnp.concatenate([rows[i * SUF : (i + 1) * SUF] for i in range(GROUP)], axis=1)
    out_ref[...] = jnp.dot(
        attended, wide_ref[...], preferred_element_type=jnp.float32
    ).astype(jnp.bfloat16)


def finish(wide, packets):
    return pl.pallas_call(
        finish_kernel,
        out_shape=jax.ShapeDtypeStruct((SUF, wide.shape[1]), jnp.bfloat16),
        compiler_params=pltpu.CompilerParams(vmem_limit_bytes=VMEM_LIMIT),
        cost_estimate=pl.CostEstimate(
            flops=2 * SUF * wide.size, bytes_accessed=2 * wide.size, transcendentals=0
        ),
        name="merge_project",
    )(wide, *packets)


def x_permute(a, step):
    pairs = [(z * NX + x, z * NX + (x + step) % NX) for z in range(NZ) for x in range(NX)]
    return lax.ppermute(a, "store", pairs)


def z_permute(a, step):
    pairs = [(z * NX + x, ((z + step) % NZ) * NX + x) for z in range(NZ) for x in range(NX)]
    return lax.ppermute(a, "store", pairs)


def y_permute(a, step):
    pairs = [
        (y * CORES + c, ((y + step) % NY) * CORES + c) for y in range(NY) for c in range(CORES)
    ]
    return lax.ppermute(a, "head", pairs)


def core_swap(a):
    return lax.ppermute(a, "head", [(h, h ^ 1) for h in range(NY * CORES)])


def sum_heads(partial):
    core = lax.rem(lax.axis_index("head"), CORES)
    y = lax.div(lax.axis_index("head"), CORES)
    parts = partial.reshape(NY, CORES, HEAD_ROWS, partial.shape[1])
    pick_core = lambda which: lax.dynamic_index_in_dim(parts, which, 1, keepdims=False)
    other = core_swap(pick_core(1 - core))
    both = pick_core(core).astype(jnp.float32) + other.astype(jnp.float32)
    pick_y = lambda step: lax.dynamic_index_in_dim(both, rem(y + step, NY), 0, keepdims=False)
    arrived = [y_permute(pick_y(step).astype(jnp.bfloat16), step) for step in (2, 1, 3)]
    return (pick_y(0) + sum(a.astype(jnp.float32) for a in arrived)).astype(jnp.bfloat16)


def local(queries, suffix_kv, kv_cache, block_owner, block_slot, prefix_blocks, out_weight):
    store_count = lax.axis_size("store")
    me = lax.axis_index("store").astype(jnp.int32).reshape(1)
    wanted = wanted_slots(prefix_blocks, block_owner, block_slot, store_count)
    table = lax.all_to_all(wanted, "store", split_axis=0, concat_axis=0, tiled=True)
    cache = keep_in_hbm(kv_cache.reshape(kv_cache.shape[0], BLK, 2 * HD))
    suffix = suffix_kv.reshape(SUF, 2 * HD)
    far, near = CHUNKS
    away = near[:-1]
    over_x = lambda blocks: [x_permute(block, k) for k, block in enumerate(blocks, 1)]
    over_z = lambda shifts, parts: [z_permute(part, s) for s, part in zip(shifts, parts)]
    far_sent, copies = pick_far(far, me, table, cache, queries)
    far_blocks = over_x(far_sent)
    near_blocks = over_x(pick_near(near, me, table, cache))
    z_groups = [[z * NX + x for z in range(NZ)] for x in range(NX)]
    z_queries = keep_in_hbm(
        lax.all_to_all(
            copies, "store", split_axis=0, concat_axis=0, tiled=True, axis_index_groups=z_groups
        )
    )
    common = (me, table, cache, z_queries)
    parts, _ = attend(far, far, *common, far_blocks, own=(queries, suffix))
    packets = over_z(far, parts) + [parts[-1]]
    parts, _ = attend(near, away, *common, near_blocks, after=packets[:1])
    packets += over_z(away, parts)
    home, (wide,) = attend(
        near, near[-1:], *common, near_blocks, after=parts[:1], weight=keep_in_hbm(out_weight)
    )
    return sum_heads(finish(wide, packets + list(home)))


def solution(mesh):
    in_specs = (
        P("store", "head"),
        P("store", "head", None),
        P("store", "head", None, None),
        P("store", None),
        P("store", None),
        P("store"),
        P("head", None),
    )
    out_specs = P(("store", "head"), None)
    return jax.shard_map(local, mesh=mesh, in_specs=in_specs, out_specs=out_specs, check_vma=False)
```

```python
import functools
import math

import jax
import jax.numpy as jnp
from jax import lax
from jax.experimental import pallas as pl
from jax.experimental.pallas import tpu as pltpu
from jax.sharding import PartitionSpec as P

HD = 128
SUF = 64
BLK = 64
CAP = 4
GROUP = 8
ROWS = SUF * GROUP
STATS = 16
PACKET = HD + STATS
NX = 4
NZ = 8
NY = 4
CORES = 2
HEAD_ROWS = SUF // (NY * CORES)

NEG_FILL = -1e30
FLOOR = -1e9
TO_LOG2 = math.log2(math.e) / math.sqrt(HD)
CHUNKS = ((4, 3, 5, 2), (6, 7, 1, 0))
WIDE_PARTS = 8
VMEM_LIMIT = 24 * 1024 * 1024

CONTRACT_LAST = (((1,), (1,)), ((), ()))
CONTRACT_FIRST = (((0,), (0,)), ((), ()))

IN_SMEM = pl.BlockSpec(memory_space=pltpu.SMEM)
IN_VMEM = pl.BlockSpec(memory_space=pltpu.VMEM)
IN_HBM = pl.BlockSpec(memory_space=pltpu.HBM)


def keep_in_hbm(a):
    return pltpu.with_memory_space_constraint(a, pltpu.HBM)


def rem(a, n):
    return lax.rem(a + n, n)


def coordinates(me_ref):
    return lax.div(me_ref[0], NX), lax.rem(me_ref[0], NX)


def wanted_kernel(length_ref, owner_hbm, slot_hbm, query_hbm, out_ref, copies_ref, *scratch):
    owner_ref, slot_ref, query_ref, sems, copy_sems = scratch
    fetches = [
        pltpu.make_async_copy(owner_hbm, owner_ref, sems.at[0]),
        pltpu.make_async_copy(slot_hbm, slot_ref, sems.at[1]),
        pltpu.make_async_copy(query_hbm, query_ref, sems.at[2]),
    ]
    for fetch in fetches:
        fetch.start()
    copies = [
        pltpu.make_async_copy(query_ref, copies_ref.at[z], copy_sems.at[z]) for z in range(NZ)
    ]
    fetches[0].wait()
    fetches[1].wait()
    count = owner_ref.shape[1]
    owners = count // CAP
    entry = lax.broadcasted_iota(jnp.int32, (1, count), 1)
    owner = jnp.where(entry < length_ref[0], owner_ref[...], owners)
    at_owner = lax.broadcasted_iota(jnp.int32, (owners, count), 0) == owner
    hits = jnp.where(at_owner, 1.0, 0.0)
    earlier = lax.broadcasted_iota(jnp.int32, (count, count), 0) < lax.broadcasted_iota(
        jnp.int32, (count, count), 1
    )
    before = jnp.dot(
        hits.astype(jnp.bfloat16),
        jnp.where(earlier, 1.0, 0.0).astype(jnp.bfloat16),
        preferred_element_type=jnp.float32,
    )
    ordinal = jnp.sum(before * hits, axis=0, keepdims=True).astype(jnp.int32)
    target = jnp.where(ordinal < CAP, owner * CAP + ordinal, count)
    chosen = jnp.where(lax.broadcasted_iota(jnp.int32, (count, count), 0) == target, 1.0, 0.0)
    slots = jnp.broadcast_to((slot_ref[...] + 1).astype(jnp.float32), (8, count))
    row = lax.dot_general(
        slots.astype(jnp.bfloat16),
        chosen.astype(jnp.bfloat16),
        CONTRACT_LAST,
        preferred_element_type=jnp.float32,
    )
    out_ref[...] = jnp.broadcast_to(
        (row[0:1].astype(jnp.int32) - 1).reshape(1, 1, count), out_ref.shape
    )
    fetches[2].wait()
    for copy in copies:
        copy.start()
    for copy in copies:
        copy.wait()


def wanted_slots(prefix_blocks, block_owner, block_slot, queries, store_count):
    return pl.pallas_call(
        wanted_kernel,
        out_shape=[
            jax.ShapeDtypeStruct((store_count, 1, block_owner.shape[1]), jnp.int32),
            jax.ShapeDtypeStruct((NZ,) + queries.shape, queries.dtype),
        ],
        in_specs=[IN_SMEM, IN_HBM, IN_HBM, IN_HBM],
        out_specs=[IN_VMEM, IN_HBM],
        scratch_shapes=[
            pltpu.VMEM(block_owner.shape, block_owner.dtype),
            pltpu.VMEM(block_slot.shape, block_slot.dtype),
            pltpu.VMEM(queries.shape, queries.dtype),
            pltpu.SemaphoreType.DMA((3,)),
            pltpu.SemaphoreType.DMA((NZ,)),
        ],
        compiler_params=pltpu.CompilerParams(vmem_limit_bytes=VMEM_LIMIT),
        name="wanted_slots",
    )(prefix_blocks, keep_in_hbm(block_owner), keep_in_hbm(block_slot), keep_in_hbm(queries))


def slot_of(table_ref, home, owner, c, cache_ref):
    return jnp.clip(table_ref[home, 0, owner * CAP + c], 0, cache_ref.shape[0] - 1)


def start_picks(shifts, k, me_ref, table_ref, cache_ref, out, sem):
    zo, xo = coordinates(me_ref)
    for n, shift in enumerate(shifts):
        home = rem(zo + shift, NZ) * NX + rem(xo + k, NX)
        for c in range(CAP):
            slot = slot_of(table_ref, home, me_ref[0], c, cache_ref)
            pltpu.make_async_copy(
                cache_ref.at[pl.ds(slot, 1)], out.at[pl.ds(n * CAP + c, 1)], sem
            ).start()


def wait_picks(shifts, cache_ref, out, sem):
    pltpu.make_async_copy(cache_ref.at[pl.ds(0, len(shifts) * CAP)], out, sem).wait()


def pick_far_kernel(shifts, me_ref, table_ref, cache_ref, *refs):
    outs, sems = refs[:-1], refs[-1]
    for k, out in enumerate(outs, 1):
        start_picks(shifts, k, me_ref, table_ref, cache_ref, out, sems.at[k - 1])
    for k, out in enumerate(outs, 1):
        wait_picks(shifts, cache_ref, out, sems.at[k - 1])


def pick_far(shifts, me, table, cache):
    block = (len(shifts) * CAP, BLK, 2 * HD)
    return pl.pallas_call(
        functools.partial(pick_far_kernel, shifts),
        out_shape=[pltpu.VMEM(block, cache.dtype)] * (NX - 1),
        in_specs=[IN_SMEM, IN_SMEM, IN_HBM],
        out_specs=[IN_VMEM] * (NX - 1),
        scratch_shapes=[pltpu.SemaphoreType.DMA((NX - 1,))],
        compiler_params=pltpu.CompilerParams(vmem_limit_bytes=VMEM_LIMIT),
        name="pick_far",
    )(me, table, cache)


def pick_near_kernel(shifts, me_ref, table_ref, cache_ref, *refs):
    outs, here, sems = refs[: NX - 1], refs[-2], refs[-1]
    for k in range(1, NX):
        start_picks(shifts, k, me_ref, table_ref, cache_ref, here.at[k - 1], sems.at[k - 1])
    moves = []
    for k, out in enumerate(outs, 1):
        wait_picks(shifts, cache_ref, here.at[k - 1], sems.at[k - 1])
        moves.append(pltpu.make_async_copy(here.at[k - 1], out, sems.at[k - 1]))
        moves[-1].start()
    for move in moves:
        move.wait()


def pick_near(shifts, me, table, cache):
    block = (len(shifts) * CAP, BLK, 2 * HD)
    return pl.pallas_call(
        functools.partial(pick_near_kernel, shifts),
        out_shape=[jax.ShapeDtypeStruct(block, cache.dtype)] * (NX - 1),
        in_specs=[IN_SMEM, IN_SMEM, IN_HBM],
        out_specs=[IN_HBM] * (NX - 1),
        scratch_shapes=[
            pltpu.VMEM((NX - 1,) + block, cache.dtype),
            pltpu.SemaphoreType.DMA((NX - 1,)),
        ],
        compiler_params=pltpu.CompilerParams(vmem_limit_bytes=VMEM_LIMIT),
        name="pick_near",
    )(me, table, cache)


def head_rows(block):
    return jnp.concatenate([block[:, i * HD : (i + 1) * HD] for i in range(GROUP)], axis=0)


def partial_sums(score_parts, value_parts):
    peak = functools.reduce(
        jnp.maximum, [jnp.max(part, axis=0, keepdims=True) for part in score_parts]
    )
    shift = jnp.maximum(peak * TO_LOG2, FLOOR).astype(jnp.bfloat16).astype(jnp.float32)
    total = jnp.zeros((1, ROWS), jnp.float32)
    acc = jnp.zeros((HD, ROWS), jnp.float32)
    for part, values in zip(score_parts, value_parts):
        expo = jnp.exp2(part * TO_LOG2 - shift)
        total += jnp.sum(expo, axis=0, keepdims=True)
        acc += lax.dot_general(
            values, expo.astype(jnp.bfloat16), CONTRACT_FIRST, preferred_element_type=jnp.float32
        )
    return shift, total, acc


def write_packet(out_ref, shift, total, acc):
    high = total.astype(jnp.bfloat16).astype(jnp.float32)
    line = lax.broadcasted_iota(jnp.int32, (STATS, ROWS), 0)
    stats = jnp.where(line == 0, shift, jnp.where(line == 1, high, jnp.where(line == 2, total - high, 0.0)))
    out_ref[:HD, :] = acc.astype(jnp.bfloat16)
    out_ref[HD:, :] = stats.astype(jnp.bfloat16)


def read_packet(ref):
    stats = ref[HD:, :].astype(jnp.float32)
    return stats[0:1], stats[1:2] + stats[2:3], ref[:HD, :].astype(jnp.float32)


def cached_part(shift, n, me_ref, table_ref, rows, blocks):
    zo, xr = coordinates(me_ref)
    home = rem(zo + shift, NZ) * NX + xr
    score_parts, value_parts = [], []
    for k in (1, 2, 3, 0):
        owner = zo * NX + rem(xr - k, NX)
        both = blocks[k][n * CAP : (n + 1) * CAP].reshape(CAP * BLK, 2 * HD)
        scores = lax.dot_general(both[:, :HD], rows, CONTRACT_LAST, preferred_element_type=jnp.float32)
        live = [
            jnp.where(
                table_ref[home, 0, owner * CAP + c] >= 0,
                scores[c * BLK : (c + 1) * BLK],
                NEG_FILL,
            )
            for c in range(CAP)
        ]
        score_parts.append(jnp.concatenate(live, axis=0))
        value_parts.append(both[:, HD:])
    return partial_sums(score_parts, value_parts)


def suffix_part(rows, both):
    scores = lax.dot_general(both[:, :HD], rows, CONTRACT_LAST, preferred_element_type=jnp.float32)
    key = lax.broadcasted_iota(jnp.int32, (SUF, ROWS), 0)
    token = lax.rem(lax.broadcasted_iota(jnp.int32, (SUF, ROWS), 1), SUF)
    return partial_sums([jnp.where(key <= token, scores, NEG_FILL)], [both[:, HD:]])


def attend_kernel(chunk, shifts, n_after, with_suffix, with_weight, *refs):
    refs = list(refs)
    take = lambda n: [refs.pop(0) for _ in range(n)]
    me_ref, table_ref, cache_ref, z_query_ref = take(4)
    arrived = take(NX - 1)
    own_refs = take(2 * with_suffix)
    take(n_after)
    weight_ref = take(1)[0] if with_weight else None
    packet_refs = take(len(shifts) + with_suffix)
    wide_ref = take(1)[0] if with_weight else None
    here, query_here, block_sems, query_sems, wide_sems = take(5)
    zo, _ = coordinates(me_ref)
    first = chunk.index(shifts[0]) * CAP
    fetches = [
        pltpu.make_async_copy(
            arrived[k - 1].at[pl.ds(first, len(shifts) * CAP)], here.at[k], block_sems.at[k]
        )
        for k in range(1, NX)
    ]
    for n, shift in enumerate(shifts):
        fetches.append(
            pltpu.make_async_copy(
                z_query_ref.at[rem(zo + shift, NZ)], query_here.at[n], query_sems.at[n]
            )
        )
    for fetch in fetches:
        fetch.start()
    start_picks(shifts, 0, me_ref, table_ref, cache_ref, here.at[0], block_sems.at[0])
    wide = []
    if with_weight:
        step = weight_ref.shape[0] // WIDE_PARTS
        for n in range(WIDE_PARTS):
            part = pl.ds(n * step, step)
            wide.append(
                pltpu.make_async_copy(weight_ref.at[part, :], wide_ref.at[part, :], wide_sems.at[n])
            )
            wide[-1].start()
    if with_suffix:
        part = suffix_part(head_rows(own_refs[0][...]), own_refs[1][...])
        write_packet(packet_refs[-1], *part)
    for fetch in fetches:
        fetch.wait()
    wait_picks(shifts, cache_ref, here.at[0], block_sems.at[0])
    for n, shift in enumerate(shifts):
        rows = head_rows(query_here[n])
        part = cached_part(shift, n, me_ref, table_ref, rows, [here.at[k] for k in range(NX)])
        write_packet(packet_refs[n], *part)
    for copy in wide:
        copy.wait()


def attend(chunk, shifts, me, table, cache, z_queries, arrived, own=(), after=(), weight=None):
    keys = len(shifts) * NX * CAP * BLK
    with_weight = weight is not None
    n_packets = len(shifts) + bool(own)
    extra = list(after) + ([weight] if with_weight else [])
    wide = [pltpu.VMEM(weight.shape, weight.dtype)] if with_weight else []
    outs = pl.pallas_call(
        functools.partial(attend_kernel, chunk, shifts, len(after), bool(own), with_weight),
        out_shape=[jax.ShapeDtypeStruct((PACKET, ROWS), jnp.bfloat16)] * n_packets + wide,
        in_specs=[IN_SMEM] * 2 + [IN_HBM] * (NX + 1) + [IN_VMEM] * len(own) + [IN_HBM] * len(extra),
        out_specs=[IN_VMEM] * (n_packets + len(wide)),
        scratch_shapes=[
            pltpu.VMEM((NX, len(shifts) * CAP, BLK, 2 * HD), cache.dtype),
            pltpu.VMEM((len(shifts), SUF, GROUP * HD), jnp.bfloat16),
            pltpu.SemaphoreType.DMA((NX,)),
            pltpu.SemaphoreType.DMA((len(shifts),)),
            pltpu.SemaphoreType.DMA((WIDE_PARTS,)),
        ],
        compiler_params=pltpu.CompilerParams(vmem_limit_bytes=VMEM_LIMIT),
        cost_estimate=pl.CostEstimate(
            flops=4 * keys * ROWS * HD, bytes_accessed=4 * keys * HD, transcendentals=keys * ROWS
        ),
        name="attend_chunk",
    )(me, table, cache, z_queries, *arrived, *own, *extra)
    return outs[:n_packets], outs[n_packets:]


def finish_kernel(wide_ref, *rest):
    packet_refs, out_ref = rest[:-1], rest[-1]
    parts = [read_packet(ref) for ref in packet_refs]
    top = functools.reduce(jnp.maximum, [part[0] for part in parts])
    factors = [jnp.exp2(part[0] - top) for part in parts]
    row_sum = sum(f * part[1] for f, part in zip(factors, parts))
    summed = sum(f * part[2] for f, part in zip(factors, parts))
    rows = (summed / row_sum).T.astype(jnp.bfloat16)
    attended = jnp.concatenate([rows[i * SUF : (i + 1) * SUF] for i in range(GROUP)], axis=1)
    out_ref[...] = jnp.dot(
        attended, wide_ref[...], preferred_element_type=jnp.float32
    ).astype(jnp.bfloat16)


def finish(wide, packets):
    return pl.pallas_call(
        finish_kernel,
        out_shape=jax.ShapeDtypeStruct((SUF, wide.shape[1]), jnp.bfloat16),
        compiler_params=pltpu.CompilerParams(vmem_limit_bytes=VMEM_LIMIT),
        cost_estimate=pl.CostEstimate(
            flops=2 * SUF * wide.size, bytes_accessed=2 * wide.size, transcendentals=0
        ),
        name="merge_project",
    )(wide, *packets)


def x_permute(a, step):
    pairs = [(z * NX + x, z * NX + (x + step) % NX) for z in range(NZ) for x in range(NX)]
    return lax.ppermute(a, "store", pairs)


def z_permute(a, step):
    pairs = [(z * NX + x, ((z + step) % NZ) * NX + x) for z in range(NZ) for x in range(NX)]
    return lax.ppermute(a, "store", pairs)


def y_permute(a, step):
    pairs = [
        (y * CORES + c, ((y + step) % NY) * CORES + c) for y in range(NY) for c in range(CORES)
    ]
    return lax.ppermute(a, "head", pairs)


def core_swap(a):
    return lax.ppermute(a, "head", [(h, h ^ 1) for h in range(NY * CORES)])


def sum_heads(partial):
    core = lax.rem(lax.axis_index("head"), CORES)
    y = lax.div(lax.axis_index("head"), CORES)
    parts = partial.reshape(NY, CORES, HEAD_ROWS, partial.shape[1])
    pick_core = lambda which: lax.dynamic_index_in_dim(parts, which, 1, keepdims=False)
    other = core_swap(pick_core(1 - core))
    both = pick_core(core).astype(jnp.float32) + other.astype(jnp.float32)
    pick_y = lambda step: lax.dynamic_index_in_dim(both, rem(y + step, NY), 0, keepdims=False)
    arrived = [y_permute(pick_y(step).astype(jnp.bfloat16), step) for step in (2, 1, 3)]
    return (pick_y(0) + sum(a.astype(jnp.float32) for a in arrived)).astype(jnp.bfloat16)


def local(queries, suffix_kv, kv_cache, block_owner, block_slot, prefix_blocks, out_weight):
    store_count = lax.axis_size("store")
    me = lax.axis_index("store").astype(jnp.int32).reshape(1)
    wanted, copies = wanted_slots(prefix_blocks, block_owner, block_slot, queries, store_count)
    table = lax.all_to_all(wanted, "store", split_axis=0, concat_axis=0, tiled=True)
    cache = keep_in_hbm(kv_cache.reshape(kv_cache.shape[0], BLK, 2 * HD))
    suffix = suffix_kv.reshape(SUF, 2 * HD)
    far, near = CHUNKS
    away = near[:-1]
    over_x = lambda blocks: [x_permute(block, k) for k, block in enumerate(blocks, 1)]
    over_z = lambda shifts, parts: [z_permute(part, s) for s, part in zip(shifts, parts)]
    far_sent = pick_far(far, me, table, cache)
    far_blocks = over_x(far_sent)
    near_blocks = over_x(pick_near(near, me, table, cache))
    z_groups = [[z * NX + x for z in range(NZ)] for x in range(NX)]
    z_queries = keep_in_hbm(
        lax.all_to_all(
            copies, "store", split_axis=0, concat_axis=0, tiled=True, axis_index_groups=z_groups
        )
    )
    common = (me, table, cache, z_queries)
    parts, _ = attend(far, far, *common, far_blocks, own=(queries, suffix))
    packets = over_z(far, parts) + [parts[-1]]
    parts, _ = attend(near, away, *common, near_blocks, after=packets[:1])
    packets += over_z(away, parts)
    home, (wide,) = attend(
        near, near[-1:], *common, near_blocks, after=parts[:1], weight=keep_in_hbm(out_weight)
    )
    return sum_heads(finish(wide, packets + list(home)))


def solution(mesh):
    in_specs = (
        P("store", "head"),
        P("store", "head", None),
        P("store", "head", None, None),
        P("store", None),
        P("store", None),
        P("store"),
        P("head", None),
    )
    out_specs = P(("store", "head"), None)
    return jax.shard_map(local, mesh=mesh, in_specs=in_specs, out_specs=out_specs, check_vma=False)
```

```python
import functools
import math

import jax
import jax.numpy as jnp
from jax import lax
from jax.experimental import pallas as pl
from jax.experimental.pallas import tpu as pltpu
from jax.sharding import PartitionSpec as P

HD = 128
SUF = 64
BLK = 64
CAP = 4
GROUP = 8
ROWS = SUF * GROUP
STATS = 16
PACKET = HD + STATS
NX = 4
NZ = 8
NY = 4
CORES = 2
HEAD_ROWS = SUF // (NY * CORES)

NEG_FILL = -1e30
FLOOR = -1e9
TO_LOG2 = math.log2(math.e) / math.sqrt(HD)
CHUNKS = ((4, 3, 5), (2, 6, 7, 1, 0))
RELAY = 2
WIDE_PARTS = 8
VMEM_LIMIT = 24 * 1024 * 1024

CONTRACT_LAST = (((1,), (1,)), ((), ()))
CONTRACT_FIRST = (((0,), (0,)), ((), ()))

IN_SMEM = pl.BlockSpec(memory_space=pltpu.SMEM)
IN_VMEM = pl.BlockSpec(memory_space=pltpu.VMEM)
IN_HBM = pl.BlockSpec(memory_space=pltpu.HBM)


def keep_in_hbm(a):
    return pltpu.with_memory_space_constraint(a, pltpu.HBM)


def rem(a, n):
    return lax.rem(a + n, n)


def coordinates(me_ref):
    return lax.div(me_ref[0], NX), lax.rem(me_ref[0], NX)


def wanted_kernel(length_ref, owner_hbm, slot_hbm, query_hbm, out_ref, copies_ref, *scratch):
    owner_ref, slot_ref, query_ref, sems, copy_sems = scratch
    fetches = [
        pltpu.make_async_copy(owner_hbm, owner_ref, sems.at[0]),
        pltpu.make_async_copy(slot_hbm, slot_ref, sems.at[1]),
        pltpu.make_async_copy(query_hbm, query_ref, sems.at[2]),
    ]
    for fetch in fetches:
        fetch.start()
    copies = [
        pltpu.make_async_copy(query_ref, copies_ref.at[z], copy_sems.at[z]) for z in range(NZ)
    ]
    for fetch in fetches:
        fetch.wait()
    for copy in copies:
        copy.start()
    count = owner_ref.shape[1]
    owners = count // CAP
    entry = lax.broadcasted_iota(jnp.int32, (1, count), 1)
    owner = jnp.where(entry < length_ref[0], owner_ref[...], owners)
    at_owner = lax.broadcasted_iota(jnp.int32, (owners, count), 0) == owner
    hits = jnp.where(at_owner, 1.0, 0.0)
    earlier = lax.broadcasted_iota(jnp.int32, (count, count), 0) < lax.broadcasted_iota(
        jnp.int32, (count, count), 1
    )
    before = jnp.dot(
        hits.astype(jnp.bfloat16),
        jnp.where(earlier, 1.0, 0.0).astype(jnp.bfloat16),
        preferred_element_type=jnp.float32,
    )
    ordinal = jnp.sum(before * hits, axis=0, keepdims=True).astype(jnp.int32)
    target = jnp.where(ordinal < CAP, owner * CAP + ordinal, count)
    chosen = jnp.where(lax.broadcasted_iota(jnp.int32, (count, count), 0) == target, 1.0, 0.0)
    slots = jnp.broadcast_to((slot_ref[...] + 1).astype(jnp.float32), (8, count))
    row = lax.dot_general(
        slots.astype(jnp.bfloat16),
        chosen.astype(jnp.bfloat16),
        CONTRACT_LAST,
        preferred_element_type=jnp.float32,
    )
    out_ref[...] = jnp.broadcast_to(
        (row[0:1].astype(jnp.int32) - 1).reshape(1, 1, count), out_ref.shape
    )
    for copy in copies:
        copy.wait()


def wanted_slots(prefix_blocks, block_owner, block_slot, queries, store_count):
    return pl.pallas_call(
        wanted_kernel,
        out_shape=[
            jax.ShapeDtypeStruct((store_count, 1, block_owner.shape[1]), jnp.int32),
            jax.ShapeDtypeStruct((NZ,) + queries.shape, queries.dtype),
        ],
        in_specs=[IN_SMEM, IN_HBM, IN_HBM, IN_HBM],
        out_specs=[IN_VMEM, IN_HBM],
        scratch_shapes=[
            pltpu.VMEM(block_owner.shape, block_owner.dtype),
            pltpu.VMEM(block_slot.shape, block_slot.dtype),
            pltpu.VMEM(queries.shape, queries.dtype),
            pltpu.SemaphoreType.DMA((3,)),
            pltpu.SemaphoreType.DMA((NZ,)),
        ],
        compiler_params=pltpu.CompilerParams(vmem_limit_bytes=VMEM_LIMIT),
        name="wanted_slots",
    )(prefix_blocks, keep_in_hbm(block_owner), keep_in_hbm(block_slot), keep_in_hbm(queries))


def slot_of(table_ref, home, owner, c, cache_ref):
    return jnp.clip(table_ref[home, 0, owner * CAP + c], 0, cache_ref.shape[0] - 1)


def start_picks(shifts, k, me_ref, table_ref, cache_ref, out, sem):
    zo, xo = coordinates(me_ref)
    for n, shift in enumerate(shifts):
        home = rem(zo + shift, NZ) * NX + rem(xo + k, NX)
        for c in range(CAP):
            slot = slot_of(table_ref, home, me_ref[0], c, cache_ref)
            pltpu.make_async_copy(
                cache_ref.at[pl.ds(slot, 1)], out.at[pl.ds(n * CAP + c, 1)], sem
            ).start()


def wait_picks(shifts, cache_ref, out, sem):
    pltpu.make_async_copy(cache_ref.at[pl.ds(0, len(shifts) * CAP)], out, sem).wait()


def pick_far_kernel(shifts, me_ref, table_ref, cache_ref, *refs):
    outs, sems = refs[:-1], refs[-1]
    for k, out in enumerate(outs, 1):
        start_picks(shifts, k, me_ref, table_ref, cache_ref, out, sems.at[k - 1])
    for k, out in enumerate(outs, 1):
        wait_picks(shifts, cache_ref, out, sems.at[k - 1])


def pick_far(shifts, me, table, cache):
    block = (len(shifts) * CAP, BLK, 2 * HD)
    return pl.pallas_call(
        functools.partial(pick_far_kernel, shifts),
        out_shape=[pltpu.VMEM(block, cache.dtype)] * (NX - 1),
        in_specs=[IN_SMEM, IN_SMEM, IN_HBM],
        out_specs=[IN_VMEM] * (NX - 1),
        scratch_shapes=[pltpu.SemaphoreType.DMA((NX - 1,))],
        compiler_params=pltpu.CompilerParams(vmem_limit_bytes=VMEM_LIMIT),
        name="pick_far",
    )(me, table, cache)


def pick_near_kernel(shifts, me_ref, table_ref, cache_ref, *refs):
    outs, here, sems = refs[: NX - 1], refs[-2], refs[-1]
    for k in range(1, NX):
        start_picks(shifts, k, me_ref, table_ref, cache_ref, here.at[k - 1], sems.at[k - 1])
    moves = []
    for k, out in enumerate(outs, 1):
        wait_picks(shifts, cache_ref, here.at[k - 1], sems.at[k - 1])
        moves.append(pltpu.make_async_copy(here.at[k - 1], out, sems.at[k - 1]))
        moves[-1].start()
    for move in moves:
        move.wait()


def pick_near(shifts, me, table, cache):
    block = (len(shifts) * CAP, BLK, 2 * HD)
    return pl.pallas_call(
        functools.partial(pick_near_kernel, shifts),
        out_shape=[jax.ShapeDtypeStruct(block, cache.dtype)] * (NX - 1),
        in_specs=[IN_SMEM, IN_SMEM, IN_HBM],
        out_specs=[IN_HBM] * (NX - 1),
        scratch_shapes=[
            pltpu.VMEM((NX - 1,) + block, cache.dtype),
            pltpu.SemaphoreType.DMA((NX - 1,)),
        ],
        compiler_params=pltpu.CompilerParams(vmem_limit_bytes=VMEM_LIMIT),
        name="pick_near",
    )(me, table, cache)


def head_rows(block):
    return jnp.concatenate([block[:, i * HD : (i + 1) * HD] for i in range(GROUP)], axis=0)


def partial_sums(scores, lives, values):
    pieces = []
    for part, live in zip(scores, lives):
        size = part.shape[0] // len(live)
        pieces.append([part[c * size : (c + 1) * size] for c in range(len(live))])
    peaks = [
        jnp.where(alive, jnp.max(piece, axis=0, keepdims=True), NEG_FILL)
        for row, live in zip(pieces, lives)
        for piece, alive in zip(row, live)
    ]
    peak = functools.reduce(jnp.maximum, peaks)
    shift = jnp.maximum(peak * TO_LOG2, FLOOR).astype(jnp.bfloat16).astype(jnp.float32)
    total = jnp.zeros((1, ROWS), jnp.float32)
    acc = jnp.zeros((HD, ROWS), jnp.float32)
    for row, live, value in zip(pieces, lives, values):
        expo = jnp.concatenate(
            [
                jnp.exp2(piece * TO_LOG2 - jnp.where(alive, shift, -NEG_FILL))
                for piece, alive in zip(row, live)
            ],
            axis=0,
        )
        total += jnp.sum(expo, axis=0, keepdims=True)
        acc += lax.dot_general(
            value, expo.astype(jnp.bfloat16), CONTRACT_FIRST, preferred_element_type=jnp.float32
        )
    return shift, total, acc


def write_packet(out_ref, shift, total, acc):
    high = total.astype(jnp.bfloat16).astype(jnp.float32)
    line = lax.broadcasted_iota(jnp.int32, (STATS, ROWS), 0)
    stats = jnp.where(line == 0, shift, jnp.where(line == 1, high, jnp.where(line == 2, total - high, 0.0)))
    out_ref[:HD, :] = acc.astype(jnp.bfloat16)
    out_ref[HD:, :] = stats.astype(jnp.bfloat16)


def merge_parts(parts):
    top = functools.reduce(jnp.maximum, [part[0] for part in parts])
    factors = [jnp.exp2(part[0] - top) for part in parts]
    total = sum(f * part[1] for f, part in zip(factors, parts))
    return top, total, sum(f * part[2] for f, part in zip(factors, parts))


def read_packet(ref):
    stats = ref[HD:, :].astype(jnp.float32)
    return stats[0:1], stats[1:2] + stats[2:3], ref[:HD, :].astype(jnp.float32)


def cached_scores(shift, n, me_ref, table_ref, rows, blocks):
    zo, xr = coordinates(me_ref)
    home = rem(zo + shift, NZ) * NX + xr
    scores, lives, values = [], [], []
    for k in (1, 2, 3, 0):
        owner = zo * NX + rem(xr - k, NX)
        both = blocks[k][n * CAP : (n + 1) * CAP].reshape(CAP * BLK, 2 * HD)
        scores.append(
            lax.dot_general(both[:, :HD], rows, CONTRACT_LAST, preferred_element_type=jnp.float32)
        )
        lives.append([table_ref[home, 0, owner * CAP + c] >= 0 for c in range(CAP)])
        values.append(both[:, HD:])
    return scores, lives, values


def suffix_part(rows, both):
    scores = lax.dot_general(both[:, :HD], rows, CONTRACT_LAST, preferred_element_type=jnp.float32)
    key = lax.broadcasted_iota(jnp.int32, (SUF, ROWS), 0)
    token = lax.rem(lax.broadcasted_iota(jnp.int32, (SUF, ROWS), 1), SUF)
    return partial_sums([jnp.where(key <= token, scores, NEG_FILL)], [[True]], [both[:, HD:]])


def attend_kernel(chunk, shifts, has, *refs):
    refs = list(refs)
    take = lambda n: [refs.pop(0) for _ in range(n)]
    me_ref, table_ref, cache_ref, z_query_ref = take(4)
    arrived = take(NX - 1)
    own_refs = take(2 * has["suffix"])
    relayed = take(2 * has["relayed"])
    weight_ref = take(2)[0] if has["weight"] else None
    packet_refs = take(2 if has["relay"] else len(shifts))
    own_packet = take(1)[0] if has["suffix"] else None
    wide_ref = take(1)[0] if has["weight"] else None
    here, query_here, block_sems, query_sems, wide_sems = take(5)
    zo, _ = coordinates(me_ref)
    wide = []
    if has["weight"]:
        step = weight_ref.shape[0] // WIDE_PARTS
        for n in range(WIDE_PARTS):
            part = pl.ds(n * step, step)
            wide.append(
                pltpu.make_async_copy(weight_ref.at[part, :], wide_ref.at[part, :], wide_sems.at[n])
            )
            wide[-1].start()
    first = chunk.index(shifts[0]) * CAP
    fetches = [
        pltpu.make_async_copy(
            arrived[k - 1].at[pl.ds(first, len(shifts) * CAP)], here.at[k], block_sems.at[k]
        )
        for k in range(1, NX)
    ]
    for n, shift in enumerate(shifts):
        fetches.append(
            pltpu.make_async_copy(
                z_query_ref.at[rem(zo + shift, NZ)], query_here.at[n], query_sems.at[n]
            )
        )
    for fetch in fetches:
        fetch.start()
    start_picks(shifts, 0, me_ref, table_ref, cache_ref, here.at[0], block_sems.at[0])
    if has["suffix"]:
        part = suffix_part(head_rows(own_refs[0][...]), own_refs[1][...])
        write_packet(own_packet, *part)
    for fetch in fetches:
        fetch.wait()
    wait_picks(shifts, cache_ref, here.at[0], block_sems.at[0])
    def scores_of(n):
        blocks = [here.at[k] for k in range(NX)]
        return cached_scores(shifts[n], n, me_ref, table_ref, head_rows(query_here[n]), blocks)

    following = scores_of(0)
    for n, shift in enumerate(shifts):
        current = following
        if n + 1 < len(shifts):
            following = scores_of(n + 1)
        part = partial_sums(*current)
        if has["relay"]:
            out = {4: packet_refs[0].at[0], 3: packet_refs[0].at[1], 5: packet_refs[1]}[shift]
        else:
            out = packet_refs[n]
        if has["relayed"] and shift in (2, 1, 7):
            other = {2: relayed[0].at[0], 1: relayed[0].at[1], 7: relayed[1]}[shift]
            part = merge_parts([part, read_packet(other)])
        write_packet(out, *part)
    for copy in wide:
        copy.wait()


def attend(chunk, shifts, me, table, cache, z_queries, arrived, own=(), relay=False, relayed=(), weight=()):
    keys = len(shifts) * NX * CAP * BLK
    has = dict(suffix=bool(own), relay=relay, relayed=bool(relayed), weight=bool(weight))
    packet = jax.ShapeDtypeStruct((PACKET, ROWS), jnp.bfloat16)
    pair = jax.ShapeDtypeStruct((2, PACKET, ROWS), jnp.bfloat16)
    packets = ([pair, packet] if relay else [packet] * len(shifts)) + [packet] * bool(own)
    wide = [pltpu.VMEM(weight[0].shape, weight[0].dtype)] if weight else []
    outs = pl.pallas_call(
        functools.partial(attend_kernel, chunk, shifts, has),
        out_shape=packets + wide,
        in_specs=[IN_SMEM] * 2
        + [IN_HBM] * (NX + 1)
        + [IN_VMEM] * (len(own) + len(relayed))
        + [IN_HBM] * len(weight),
        out_specs=[IN_VMEM] * len(packets + wide),
        scratch_shapes=[
            pltpu.VMEM((NX, len(shifts) * CAP, BLK, 2 * HD), cache.dtype),
            pltpu.VMEM((len(shifts), SUF, GROUP * HD), jnp.bfloat16),
            pltpu.SemaphoreType.DMA((NX,)),
            pltpu.SemaphoreType.DMA((len(shifts),)),
            pltpu.SemaphoreType.DMA((WIDE_PARTS,)),
        ],
        compiler_params=pltpu.CompilerParams(vmem_limit_bytes=VMEM_LIMIT),
        cost_estimate=pl.CostEstimate(
            flops=4 * keys * ROWS * HD, bytes_accessed=4 * keys * HD, transcendentals=keys * ROWS
        ),
        name="attend_chunk",
    )(me, table, cache, z_queries, *arrived, *own, *relayed, *weight)
    return outs


def finish_kernel(wide_ref, *rest):
    packet_refs, out_ref = rest[:-1], rest[-1]
    _, row_sum, summed = merge_parts([read_packet(ref) for ref in packet_refs])
    rows = (summed / row_sum).T.astype(jnp.bfloat16)
    attended = jnp.concatenate([rows[i * SUF : (i + 1) * SUF] for i in range(GROUP)], axis=1)
    out_ref[...] = jnp.dot(
        attended, wide_ref[...], preferred_element_type=jnp.float32
    ).astype(jnp.bfloat16)


def finish(wide, packets):
    return pl.pallas_call(
        finish_kernel,
        out_shape=jax.ShapeDtypeStruct((SUF, wide.shape[1]), jnp.bfloat16),
        compiler_params=pltpu.CompilerParams(vmem_limit_bytes=VMEM_LIMIT),
        cost_estimate=pl.CostEstimate(
            flops=2 * SUF * wide.size, bytes_accessed=2 * wide.size, transcendentals=0
        ),
        name="merge_project",
    )(wide, *packets)


def x_permute(a, step):
    pairs = [(z * NX + x, z * NX + (x + step) % NX) for z in range(NZ) for x in range(NX)]
    return lax.ppermute(a, "store", pairs)


def z_permute(a, step):
    pairs = [(z * NX + x, ((z + step) % NZ) * NX + x) for z in range(NZ) for x in range(NX)]
    return lax.ppermute(a, "store", pairs)


def y_permute(a, step):
    pairs = [
        (y * CORES + c, ((y + step) % NY) * CORES + c) for y in range(NY) for c in range(CORES)
    ]
    return lax.ppermute(a, "head", pairs)


def core_swap(a):
    return lax.ppermute(a, "head", [(h, h ^ 1) for h in range(NY * CORES)])


def sum_heads(partial):
    core = lax.rem(lax.axis_index("head"), CORES)
    y = lax.div(lax.axis_index("head"), CORES)
    parts = partial.reshape(NY, CORES, HEAD_ROWS, partial.shape[1])
    pick_core = lambda which: lax.dynamic_index_in_dim(parts, which, 1, keepdims=False)
    other = core_swap(pick_core(1 - core))
    both = pick_core(core).astype(jnp.float32) + other.astype(jnp.float32)
    pick_y = lambda step: lax.dynamic_index_in_dim(both, rem(y + step, NY), 0, keepdims=False)
    arrived = [y_permute(pick_y(step).astype(jnp.bfloat16), step) for step in (2, 1, 3)]
    return (pick_y(0) + sum(a.astype(jnp.float32) for a in arrived)).astype(jnp.bfloat16)


def local(queries, suffix_kv, kv_cache, block_owner, block_slot, prefix_blocks, out_weight):
    store_count = lax.axis_size("store")
    me = lax.axis_index("store").astype(jnp.int32).reshape(1)
    wanted, copies = wanted_slots(prefix_blocks, block_owner, block_slot, queries, store_count)
    table = lax.all_to_all(wanted, "store", split_axis=0, concat_axis=0, tiled=True)
    cache = keep_in_hbm(kv_cache.reshape(kv_cache.shape[0], BLK, 2 * HD))
    suffix = suffix_kv.reshape(SUF, 2 * HD)
    far, near = CHUNKS
    away = near[:-1]
    over_x = lambda blocks: [x_permute(block, k) for k, block in enumerate(blocks, 1)]
    over_z = lambda shifts, parts: [z_permute(part, s) for s, part in zip(shifts, parts)]
    far_sent = pick_far(far, me, table, cache)
    far_blocks = over_x(far_sent)
    near_blocks = over_x(pick_near(near, me, table, cache))
    z_groups = [[z * NX + x for z in range(NZ)] for x in range(NX)]
    z_queries = keep_in_hbm(
        lax.all_to_all(
            copies, "store", split_axis=0, concat_axis=0, tiled=True, axis_index_groups=z_groups
        )
    )
    common = (me, table, cache, z_queries)
    plus, minus, own = attend(far, far, *common, far_blocks, own=(queries, suffix), relay=True)
    relayed = (z_permute(plus, RELAY), z_permute(minus, -RELAY))
    parts = attend(near, away, *common, near_blocks, relayed=relayed)
    packets = over_z(away, parts) + [own]
    home, wide = attend(
        near, near[-1:], *common, near_blocks, weight=(keep_in_hbm(out_weight), parts[0])
    )
    return sum_heads(finish(wide, packets + [home]))


def solution(mesh):
    in_specs = (
        P("store", "head"),
        P("store", "head", None),
        P("store", "head", None, None),
        P("store", None),
        P("store", None),
        P("store"),
        P("head", None),
    )
    out_specs = P(("store", "head"), None)
    return jax.shard_map(local, mesh=mesh, in_specs=in_specs, out_specs=out_specs, check_vma=False)
```

```python
import functools
import math

import jax
import jax.numpy as jnp
from jax import lax
from jax.experimental import pallas as pl
from jax.experimental.pallas import tpu as pltpu
from jax.sharding import PartitionSpec as P

HD = 128
SUF = 64
BLK = 64
CAP = 4
GROUP = 8
ROWS = SUF * GROUP
STATS = 16
PACKET = HD + STATS
NX = 4
NZ = 8
NY = 4
CORES = 2
HEAD_ROWS = SUF // (NY * CORES)

NEG_FILL = -1e30
FLOOR = -1e9
TO_LOG2 = math.log2(math.e) / math.sqrt(HD)
CHUNKS = ((4, 3, 5), (2, 6, 7, 1, 0))
RELAY = 2
WIDE_PARTS = 8
VMEM_LIMIT = 24 * 1024 * 1024

CONTRACT_LAST = (((1,), (1,)), ((), ()))
CONTRACT_FIRST = (((0,), (0,)), ((), ()))

IN_SMEM = pl.BlockSpec(memory_space=pltpu.SMEM)
IN_VMEM = pl.BlockSpec(memory_space=pltpu.VMEM)
IN_HBM = pl.BlockSpec(memory_space=pltpu.HBM)


def keep_in_hbm(a):
    return pltpu.with_memory_space_constraint(a, pltpu.HBM)


def rem(a, n):
    return lax.rem(a + n, n)


def coordinates(me_ref):
    return lax.div(me_ref[0], NX), lax.rem(me_ref[0], NX)


def wanted_kernel(length_ref, owner_hbm, slot_hbm, query_hbm, out_ref, copies_ref, *scratch):
    owner_ref, slot_ref, query_ref, sems, copy_sems = scratch
    fetches = [
        pltpu.make_async_copy(owner_hbm, owner_ref, sems.at[0]),
        pltpu.make_async_copy(slot_hbm, slot_ref, sems.at[1]),
        pltpu.make_async_copy(query_hbm, query_ref, sems.at[2]),
    ]
    for fetch in fetches:
        fetch.start()
    copies = [
        pltpu.make_async_copy(query_ref, copies_ref.at[z], copy_sems.at[z]) for z in range(NZ)
    ]
    for fetch in fetches:
        fetch.wait()
    for copy in copies:
        copy.start()
    count = owner_ref.shape[1]
    owners = count // CAP
    entry = lax.broadcasted_iota(jnp.int32, (1, count), 1)
    owner = jnp.where(entry < length_ref[0], owner_ref[...], owners)
    at_owner = lax.broadcasted_iota(jnp.int32, (owners, count), 0) == owner
    hits = jnp.where(at_owner, 1.0, 0.0)
    earlier = lax.broadcasted_iota(jnp.int32, (count, count), 0) < lax.broadcasted_iota(
        jnp.int32, (count, count), 1
    )
    before = jnp.dot(
        hits.astype(jnp.bfloat16),
        jnp.where(earlier, 1.0, 0.0).astype(jnp.bfloat16),
        preferred_element_type=jnp.float32,
    )
    ordinal = jnp.sum(before * hits, axis=0, keepdims=True).astype(jnp.int32)
    target = jnp.where(ordinal < CAP, owner * CAP + ordinal, count)
    chosen = jnp.where(lax.broadcasted_iota(jnp.int32, (count, count), 0) == target, 1.0, 0.0)
    slots = jnp.broadcast_to((slot_ref[...] + 1).astype(jnp.float32), (8, count))
    row = lax.dot_general(
        slots.astype(jnp.bfloat16),
        chosen.astype(jnp.bfloat16),
        CONTRACT_LAST,
        preferred_element_type=jnp.float32,
    )
    out_ref[...] = jnp.broadcast_to(
        (row[0:1].astype(jnp.int32) - 1).reshape(1, 1, count), out_ref.shape
    )
    for copy in copies:
        copy.wait()


def wanted_slots(prefix_blocks, block_owner, block_slot, queries, store_count):
    return pl.pallas_call(
        wanted_kernel,
        out_shape=[
            jax.ShapeDtypeStruct((store_count, 1, block_owner.shape[1]), jnp.int32),
            jax.ShapeDtypeStruct((NZ,) + queries.shape, queries.dtype),
        ],
        in_specs=[IN_SMEM, IN_HBM, IN_HBM, IN_HBM],
        out_specs=[IN_VMEM, IN_HBM],
        scratch_shapes=[
            pltpu.VMEM(block_owner.shape, block_owner.dtype),
            pltpu.VMEM(block_slot.shape, block_slot.dtype),
            pltpu.VMEM(queries.shape, queries.dtype),
            pltpu.SemaphoreType.DMA((3,)),
            pltpu.SemaphoreType.DMA((NZ,)),
        ],
        compiler_params=pltpu.CompilerParams(vmem_limit_bytes=VMEM_LIMIT),
        name="wanted_slots",
    )(prefix_blocks, keep_in_hbm(block_owner), keep_in_hbm(block_slot), keep_in_hbm(queries))


def slot_of(table_ref, home, owner, c, cache_ref):
    return jnp.clip(table_ref[home, 0, owner * CAP + c], 0, cache_ref.shape[0] - 1)


def start_picks(shifts, k, me_ref, table_ref, cache_ref, out, sem):
    zo, xo = coordinates(me_ref)
    for n, shift in enumerate(shifts):
        home = rem(zo + shift, NZ) * NX + rem(xo + k, NX)
        for c in range(CAP):
            slot = slot_of(table_ref, home, me_ref[0], c, cache_ref)
            pltpu.make_async_copy(
                cache_ref.at[pl.ds(slot, 1)], out.at[pl.ds(n * CAP + c, 1)], sem
            ).start()


def wait_picks(shifts, cache_ref, out, sem):
    pltpu.make_async_copy(cache_ref.at[pl.ds(0, len(shifts) * CAP)], out, sem).wait()


def pick_far_kernel(shifts, me_ref, table_ref, cache_ref, *refs):
    outs, sems = refs[:-1], refs[-1]
    for k, out in enumerate(outs, 1):
        start_picks(shifts, k, me_ref, table_ref, cache_ref, out, sems.at[k - 1])
    for k, out in enumerate(outs, 1):
        wait_picks(shifts, cache_ref, out, sems.at[k - 1])


def pick_far(shifts, me, table, cache):
    block = (len(shifts) * CAP, BLK, 2 * HD)
    return pl.pallas_call(
        functools.partial(pick_far_kernel, shifts),
        out_shape=[pltpu.VMEM(block, cache.dtype)] * (NX - 1),
        in_specs=[IN_SMEM, IN_SMEM, IN_HBM],
        out_specs=[IN_VMEM] * (NX - 1),
        scratch_shapes=[pltpu.SemaphoreType.DMA((NX - 1,))],
        compiler_params=pltpu.CompilerParams(vmem_limit_bytes=VMEM_LIMIT),
        name="pick_far",
    )(me, table, cache)


def pick_near_kernel(shifts, me_ref, table_ref, cache_ref, *refs):
    outs, here, sems = refs[: NX - 1], refs[-2], refs[-1]
    for k in range(1, NX):
        start_picks(shifts, k, me_ref, table_ref, cache_ref, here.at[k - 1], sems.at[k - 1])
    moves = []
    for k, out in enumerate(outs, 1):
        wait_picks(shifts, cache_ref, here.at[k - 1], sems.at[k - 1])
        moves.append(pltpu.make_async_copy(here.at[k - 1], out, sems.at[k - 1]))
        moves[-1].start()
    for move in moves:
        move.wait()


def pick_near(shifts, me, table, cache):
    block = (len(shifts) * CAP, BLK, 2 * HD)
    return pl.pallas_call(
        functools.partial(pick_near_kernel, shifts),
        out_shape=[jax.ShapeDtypeStruct(block, cache.dtype)] * (NX - 1),
        in_specs=[IN_SMEM, IN_SMEM, IN_HBM],
        out_specs=[IN_HBM] * (NX - 1),
        scratch_shapes=[
            pltpu.VMEM((NX - 1,) + block, cache.dtype),
            pltpu.SemaphoreType.DMA((NX - 1,)),
        ],
        compiler_params=pltpu.CompilerParams(vmem_limit_bytes=VMEM_LIMIT),
        name="pick_near",
    )(me, table, cache)


def head_rows(block):
    return jnp.concatenate([block[:, i * HD : (i + 1) * HD] for i in range(GROUP)], axis=0)


def partial_sums(scores, lives, values):
    pieces = []
    for part, live in zip(scores, lives):
        size = part.shape[0] // len(live)
        pieces.append([part[c * size : (c + 1) * size] for c in range(len(live))])
    peaks = [
        jnp.where(alive, jnp.max(piece, axis=0, keepdims=True), NEG_FILL)
        for row, live in zip(pieces, lives)
        for piece, alive in zip(row, live)
    ]
    peak = functools.reduce(jnp.maximum, peaks)
    shift = jnp.maximum(peak * TO_LOG2, FLOOR).astype(jnp.bfloat16).astype(jnp.float32)
    total = jnp.zeros((1, ROWS), jnp.float32)
    acc = jnp.zeros((HD, ROWS), jnp.float32)
    for row, live, value in zip(pieces, lives, values):
        expo = jnp.concatenate(
            [
                jnp.exp2(piece * TO_LOG2 - jnp.where(alive, shift, -NEG_FILL))
                for piece, alive in zip(row, live)
            ],
            axis=0,
        )
        total += jnp.sum(expo, axis=0, keepdims=True)
        acc += lax.dot_general(
            value, expo.astype(jnp.bfloat16), CONTRACT_FIRST, preferred_element_type=jnp.float32
        )
    return shift, total, acc


def write_packet(out_ref, shift, total, acc):
    high = total.astype(jnp.bfloat16).astype(jnp.float32)
    line = lax.broadcasted_iota(jnp.int32, (STATS, ROWS), 0)
    stats = jnp.where(line == 0, shift, jnp.where(line == 1, high, jnp.where(line == 2, total - high, 0.0)))
    out_ref[:HD, :] = acc.astype(jnp.bfloat16)
    out_ref[HD:, :] = stats.astype(jnp.bfloat16)


def merge_parts(parts):
    top = functools.reduce(jnp.maximum, [part[0] for part in parts])
    factors = [jnp.exp2(part[0] - top) for part in parts]
    total = sum(f * part[1] for f, part in zip(factors, parts))
    return top, total, sum(f * part[2] for f, part in zip(factors, parts))


def read_packet(ref):
    stats = ref[HD:, :].astype(jnp.float32)
    return stats[0:1], stats[1:2] + stats[2:3], ref[:HD, :].astype(jnp.float32)


def cached_scores(shift, me_ref, table_ref, rows, blocks):
    zo, xr = coordinates(me_ref)
    home = rem(zo + shift, NZ) * NX + xr
    scores, lives, values = [], [], []
    for k in (1, 2, 3, 0):
        owner = zo * NX + rem(xr - k, NX)
        both = blocks[k].reshape(CAP * BLK, 2 * HD)
        scores.append(
            lax.dot_general(both[:, :HD], rows, CONTRACT_LAST, preferred_element_type=jnp.float32)
        )
        lives.append([table_ref[home, 0, owner * CAP + c] >= 0 for c in range(CAP)])
        values.append(both[:, HD:])
    return scores, lives, values


def suffix_part(rows, both):
    scores = lax.dot_general(both[:, :HD], rows, CONTRACT_LAST, preferred_element_type=jnp.float32)
    key = lax.broadcasted_iota(jnp.int32, (SUF, ROWS), 0)
    token = lax.rem(lax.broadcasted_iota(jnp.int32, (SUF, ROWS), 1), SUF)
    return partial_sums([jnp.where(key <= token, scores, NEG_FILL)], [[True]], [both[:, HD:]])


def attend_kernel(chunk, shifts, has, *refs):
    refs = list(refs)
    take = lambda n: [refs.pop(0) for _ in range(n)]
    me_ref, table_ref, cache_ref, z_query_ref = take(4)
    arrived = take(NX - 1)
    own_refs = take(2 * has["suffix"])
    relayed = take(2 * has["relayed"])
    weight_ref = take(2)[0] if has["weight"] else None
    packet_refs = take(2 if has["relay"] else len(shifts))
    own_packet = take(1)[0] if has["suffix"] else None
    wide_ref = take(1)[0] if has["weight"] else None
    here, query_here, block_sem, query_sems, wide_sems = take(5)
    zo, _ = coordinates(me_ref)
    wide = []
    if has["weight"]:
        step = weight_ref.shape[0] // WIDE_PARTS
        for n in range(WIDE_PARTS):
            part = pl.ds(n * step, step)
            wide.append(
                pltpu.make_async_copy(weight_ref.at[part, :], wide_ref.at[part, :], wide_sems.at[n])
            )
            wide[-1].start()
    first = chunk.index(shifts[0])
    fetches = [
        pltpu.make_async_copy(
            z_query_ref.at[rem(zo + shift, NZ)], query_here.at[n], query_sems.at[n]
        )
        for n, shift in enumerate(shifts)
    ]
    for fetch in fetches:
        fetch.start()
    start_picks(shifts, 0, me_ref, table_ref, cache_ref, here, block_sem)
    if has["suffix"]:
        part = suffix_part(head_rows(own_refs[0][...]), own_refs[1][...])
        write_packet(own_packet, *part)
    for fetch in fetches:
        fetch.wait()
    wait_picks(shifts, cache_ref, here, block_sem)
    def scores_of(n):
        there = slice((first + n) * CAP, (first + n + 1) * CAP)
        blocks = [here[n * CAP : (n + 1) * CAP]] + [ref[there] for ref in arrived]
        return cached_scores(shifts[n], me_ref, table_ref, head_rows(query_here[n]), blocks)

    following = scores_of(0)
    for n, shift in enumerate(shifts):
        current = following
        if n + 1 < len(shifts):
            following = scores_of(n + 1)
        part = partial_sums(*current)
        if has["relay"]:
            out = {4: packet_refs[0].at[0], 3: packet_refs[0].at[1], 5: packet_refs[1]}[shift]
        else:
            out = packet_refs[n]
        if has["relayed"] and shift in (2, 1, 7):
            other = {2: relayed[0].at[0], 1: relayed[0].at[1], 7: relayed[1]}[shift]
            part = merge_parts([part, read_packet(other)])
        write_packet(out, *part)
    for copy in wide:
        copy.wait()


def attend(chunk, shifts, me, table, cache, z_queries, arrived, own=(), relay=False, relayed=(), weight=()):
    keys = len(shifts) * NX * CAP * BLK
    has = dict(suffix=bool(own), relay=relay, relayed=bool(relayed), weight=bool(weight))
    packet = jax.ShapeDtypeStruct((PACKET, ROWS), jnp.bfloat16)
    pair = jax.ShapeDtypeStruct((2, PACKET, ROWS), jnp.bfloat16)
    packets = ([pair, packet] if relay else [packet] * len(shifts)) + [packet] * bool(own)
    wide = [pltpu.VMEM(weight[0].shape, weight[0].dtype)] if weight else []
    outs = pl.pallas_call(
        functools.partial(attend_kernel, chunk, shifts, has),
        out_shape=packets + wide,
        in_specs=[IN_SMEM] * 2
        + [IN_HBM] * 2
        + [IN_VMEM] * (NX - 1 + len(own) + len(relayed))
        + [IN_HBM] * len(weight),
        out_specs=[IN_VMEM] * len(packets + wide),
        scratch_shapes=[
            pltpu.VMEM((len(shifts) * CAP, BLK, 2 * HD), cache.dtype),
            pltpu.VMEM((len(shifts), SUF, GROUP * HD), jnp.bfloat16),
            pltpu.SemaphoreType.DMA,
            pltpu.SemaphoreType.DMA((len(shifts),)),
            pltpu.SemaphoreType.DMA((WIDE_PARTS,)),
        ],
        compiler_params=pltpu.CompilerParams(vmem_limit_bytes=VMEM_LIMIT),
        cost_estimate=pl.CostEstimate(
            flops=4 * keys * ROWS * HD, bytes_accessed=4 * keys * HD, transcendentals=keys * ROWS
        ),
        name="attend_chunk",
    )(me, table, cache, z_queries, *arrived, *own, *relayed, *weight)
    return outs


def finish_kernel(wide_ref, *rest):
    packet_refs, out_ref = rest[:-1], rest[-1]
    _, row_sum, summed = merge_parts([read_packet(ref) for ref in packet_refs])
    rows = (summed / row_sum).T.astype(jnp.bfloat16)
    attended = jnp.concatenate([rows[i * SUF : (i + 1) * SUF] for i in range(GROUP)], axis=1)
    out_ref[...] = jnp.dot(
        attended, wide_ref[...], preferred_element_type=jnp.float32
    ).astype(jnp.bfloat16)


def finish(wide, packets):
    return pl.pallas_call(
        finish_kernel,
        out_shape=jax.ShapeDtypeStruct((SUF, wide.shape[1]), jnp.bfloat16),
        compiler_params=pltpu.CompilerParams(vmem_limit_bytes=VMEM_LIMIT),
        cost_estimate=pl.CostEstimate(
            flops=2 * SUF * wide.size, bytes_accessed=2 * wide.size, transcendentals=0
        ),
        name="merge_project",
    )(wide, *packets)


def x_permute(a, step):
    pairs = [(z * NX + x, z * NX + (x + step) % NX) for z in range(NZ) for x in range(NX)]
    return lax.ppermute(a, "store", pairs)


def z_permute(a, step):
    pairs = [(z * NX + x, ((z + step) % NZ) * NX + x) for z in range(NZ) for x in range(NX)]
    return lax.ppermute(a, "store", pairs)


def y_permute(a, step):
    pairs = [
        (y * CORES + c, ((y + step) % NY) * CORES + c) for y in range(NY) for c in range(CORES)
    ]
    return lax.ppermute(a, "head", pairs)


def core_swap(a):
    return lax.ppermute(a, "head", [(h, h ^ 1) for h in range(NY * CORES)])


def sum_heads(partial):
    core = lax.rem(lax.axis_index("head"), CORES)
    y = lax.div(lax.axis_index("head"), CORES)
    parts = partial.reshape(NY, CORES, HEAD_ROWS, partial.shape[1])
    pick_core = lambda which: lax.dynamic_index_in_dim(parts, which, 1, keepdims=False)
    other = core_swap(pick_core(1 - core))
    both = pick_core(core).astype(jnp.float32) + other.astype(jnp.float32)
    pick_y = lambda step: lax.dynamic_index_in_dim(both, rem(y + step, NY), 0, keepdims=False)
    arrived = [y_permute(pick_y(step).astype(jnp.bfloat16), step) for step in (2, 1, 3)]
    return (pick_y(0) + sum(a.astype(jnp.float32) for a in arrived)).astype(jnp.bfloat16)


def local(queries, suffix_kv, kv_cache, block_owner, block_slot, prefix_blocks, out_weight):
    store_count = lax.axis_size("store")
    me = lax.axis_index("store").astype(jnp.int32).reshape(1)
    wanted, copies = wanted_slots(prefix_blocks, block_owner, block_slot, queries, store_count)
    table = lax.all_to_all(wanted, "store", split_axis=0, concat_axis=0, tiled=True)
    cache = keep_in_hbm(kv_cache.reshape(kv_cache.shape[0], BLK, 2 * HD))
    suffix = suffix_kv.reshape(SUF, 2 * HD)
    far, near = CHUNKS
    away = near[:-1]
    over_x = lambda blocks: [x_permute(block, k) for k, block in enumerate(blocks, 1)]
    over_z = lambda shifts, parts: [z_permute(part, s) for s, part in zip(shifts, parts)]
    far_sent = pick_far(far, me, table, cache)
    far_blocks = over_x(far_sent)
    near_blocks = over_x(pick_near(near, me, table, cache))
    z_groups = [[z * NX + x for z in range(NZ)] for x in range(NX)]
    z_queries = keep_in_hbm(
        lax.all_to_all(
            copies, "store", split_axis=0, concat_axis=0, tiled=True, axis_index_groups=z_groups
        )
    )
    common = (me, table, cache, z_queries)
    plus, minus, own = attend(far, far, *common, far_blocks, own=(queries, suffix), relay=True)
    relayed = (z_permute(plus, RELAY), z_permute(minus, -RELAY))
    parts = attend(near, away, *common, near_blocks, relayed=relayed)
    packets = over_z(away, parts) + [own]
    home, wide = attend(
        near, near[-1:], *common, near_blocks, weight=(keep_in_hbm(out_weight), parts[0])
    )
    return sum_heads(finish(wide, packets + [home]))


def solution(mesh):
    in_specs = (
        P("store", "head"),
        P("store", "head", None),
        P("store", "head", None, None),
        P("store", None),
        P("store", None),
        P("store"),
        P("head", None),
    )
    out_specs = P(("store", "head"), None)
    return jax.shard_map(local, mesh=mesh, in_specs=in_specs, out_specs=out_specs, check_vma=False)
```

```python
import functools
import math

import jax
import jax.numpy as jnp
from jax import lax
from jax.experimental import pallas as pl
from jax.experimental.pallas import tpu as pltpu
from jax.sharding import PartitionSpec as P

HD = 128
SUF = 64
BLK = 64
CAP = 4
GROUP = 8
ROWS = SUF * GROUP
STATS = 16
PACKET = HD + STATS
NX = 4
NZ = 8
NY = 4
CORES = 2
HEAD_ROWS = SUF // (NY * CORES)

NEG_FILL = -1e30
FLOOR = -1e9
TO_LOG2 = math.log2(math.e) / math.sqrt(HD)
CHUNKS = ((4, 3, 5), (2, 6, 7, 1, 0))
RELAY = 2
WIDE_PARTS = 8
VMEM_LIMIT = 24 * 1024 * 1024

CONTRACT_LAST = (((1,), (1,)), ((), ()))
CONTRACT_FIRST = (((0,), (0,)), ((), ()))

IN_SMEM = pl.BlockSpec(memory_space=pltpu.SMEM)
IN_VMEM = pl.BlockSpec(memory_space=pltpu.VMEM)
IN_HBM = pl.BlockSpec(memory_space=pltpu.HBM)


def keep_in_hbm(a):
    return pltpu.with_memory_space_constraint(a, pltpu.HBM)


def rem(a, n):
    return lax.rem(a + n, n)


def coordinates(me_ref):
    return lax.div(me_ref[0], NX), lax.rem(me_ref[0], NX)


def wanted_kernel(length_ref, owner_hbm, slot_hbm, query_hbm, out_ref, copies_ref, *scratch):
    owner_ref, slot_ref, query_ref, sems, copy_sems = scratch
    fetches = [
        pltpu.make_async_copy(owner_hbm, owner_ref, sems.at[0]),
        pltpu.make_async_copy(slot_hbm, slot_ref, sems.at[1]),
        pltpu.make_async_copy(query_hbm, query_ref, sems.at[2]),
    ]
    for fetch in fetches:
        fetch.start()
    copies = [
        pltpu.make_async_copy(query_ref, copies_ref.at[z], copy_sems.at[z]) for z in range(NZ)
    ]
    for fetch in fetches:
        fetch.wait()
    for copy in copies:
        copy.start()
    count = owner_ref.shape[1]
    owners = count // CAP
    entry = lax.broadcasted_iota(jnp.int32, (1, count), 1)
    owner = jnp.where(entry < length_ref[0], owner_ref[...], owners)
    at_owner = lax.broadcasted_iota(jnp.int32, (owners, count), 0) == owner
    hits = jnp.where(at_owner, 1.0, 0.0)
    earlier = lax.broadcasted_iota(jnp.int32, (count, count), 0) < lax.broadcasted_iota(
        jnp.int32, (count, count), 1
    )
    before = jnp.dot(
        hits.astype(jnp.bfloat16),
        jnp.where(earlier, 1.0, 0.0).astype(jnp.bfloat16),
        preferred_element_type=jnp.float32,
    )
    ordinal = jnp.sum(before * hits, axis=0, keepdims=True).astype(jnp.int32)
    target = jnp.where(ordinal < CAP, owner * CAP + ordinal, count)
    chosen = jnp.where(lax.broadcasted_iota(jnp.int32, (count, count), 0) == target, 1.0, 0.0)
    slots = jnp.broadcast_to((slot_ref[...] + 1).astype(jnp.float32), (8, count))
    row = lax.dot_general(
        slots.astype(jnp.bfloat16),
        chosen.astype(jnp.bfloat16),
        CONTRACT_LAST,
        preferred_element_type=jnp.float32,
    )
    out_ref[...] = jnp.broadcast_to(
        (row[0:1].astype(jnp.int32) - 1).reshape(1, 1, count), out_ref.shape
    )
    for copy in copies:
        copy.wait()


def wanted_slots(prefix_blocks, block_owner, block_slot, queries, store_count):
    return pl.pallas_call(
        wanted_kernel,
        out_shape=[
            jax.ShapeDtypeStruct((store_count, 1, block_owner.shape[1]), jnp.int32),
            jax.ShapeDtypeStruct((NZ,) + queries.shape, queries.dtype),
        ],
        in_specs=[IN_SMEM, IN_HBM, IN_HBM, IN_HBM],
        out_specs=[IN_VMEM, IN_HBM],
        scratch_shapes=[
            pltpu.VMEM(block_owner.shape, block_owner.dtype),
            pltpu.VMEM(block_slot.shape, block_slot.dtype),
            pltpu.VMEM(queries.shape, queries.dtype),
            pltpu.SemaphoreType.DMA((3,)),
            pltpu.SemaphoreType.DMA((NZ,)),
        ],
        compiler_params=pltpu.CompilerParams(vmem_limit_bytes=VMEM_LIMIT),
        name="wanted_slots",
    )(prefix_blocks, keep_in_hbm(block_owner), keep_in_hbm(block_slot), keep_in_hbm(queries))


def slot_of(table_ref, home, owner, c, cache_ref):
    return jnp.clip(table_ref[home, 0, owner * CAP + c], 0, cache_ref.shape[0] - 1)


def start_picks(shifts, k, me_ref, table_ref, cache_ref, out, sem):
    zo, xo = coordinates(me_ref)
    for n, shift in enumerate(shifts):
        home = rem(zo + shift, NZ) * NX + rem(xo + k, NX)
        for c in range(CAP):
            slot = slot_of(table_ref, home, me_ref[0], c, cache_ref)
            pltpu.make_async_copy(
                cache_ref.at[pl.ds(slot, 1)], out.at[pl.ds(n * CAP + c, 1)], sem
            ).start()


def wait_picks(shifts, cache_ref, out, sem):
    pltpu.make_async_copy(cache_ref.at[pl.ds(0, len(shifts) * CAP)], out, sem).wait()


def pick_far_kernel(shifts, me_ref, table_ref, cache_ref, *refs):
    outs, sems = refs[:-1], refs[-1]
    for k, out in enumerate(outs, 1):
        start_picks(shifts, k, me_ref, table_ref, cache_ref, out, sems.at[k - 1])
    for k, out in enumerate(outs, 1):
        wait_picks(shifts, cache_ref, out, sems.at[k - 1])


def pick_far(shifts, me, table, cache):
    block = (len(shifts) * CAP, BLK, 2 * HD)
    return pl.pallas_call(
        functools.partial(pick_far_kernel, shifts),
        out_shape=[pltpu.VMEM(block, cache.dtype)] * (NX - 1),
        in_specs=[IN_SMEM, IN_SMEM, IN_HBM],
        out_specs=[IN_VMEM] * (NX - 1),
        scratch_shapes=[pltpu.SemaphoreType.DMA((NX - 1,))],
        compiler_params=pltpu.CompilerParams(vmem_limit_bytes=VMEM_LIMIT),
        name="pick_far",
    )(me, table, cache)


def pick_near_kernel(shifts, me_ref, table_ref, cache_ref, *refs):
    outs, here, sems = refs[: NX - 1], refs[-2], refs[-1]
    for k in range(1, NX):
        start_picks(shifts, k, me_ref, table_ref, cache_ref, here.at[k - 1], sems.at[k - 1])
    moves = []
    for k, out in enumerate(outs, 1):
        wait_picks(shifts, cache_ref, here.at[k - 1], sems.at[k - 1])
        moves.append(pltpu.make_async_copy(here.at[k - 1], out, sems.at[k - 1]))
        moves[-1].start()
    for move in moves:
        move.wait()


def pick_near(shifts, me, table, cache):
    block = (len(shifts) * CAP, BLK, 2 * HD)
    return pl.pallas_call(
        functools.partial(pick_near_kernel, shifts),
        out_shape=[jax.ShapeDtypeStruct(block, cache.dtype)] * (NX - 1),
        in_specs=[IN_SMEM, IN_SMEM, IN_HBM],
        out_specs=[IN_HBM] * (NX - 1),
        scratch_shapes=[
            pltpu.VMEM((NX - 1,) + block, cache.dtype),
            pltpu.SemaphoreType.DMA((NX - 1,)),
        ],
        compiler_params=pltpu.CompilerParams(vmem_limit_bytes=VMEM_LIMIT),
        name="pick_near",
    )(me, table, cache)


def head_rows(block):
    return jnp.concatenate([block[:, i * HD : (i + 1) * HD] for i in range(GROUP)], axis=0)


def partial_sums(scores, lives, values):
    pieces = []
    for part, live in zip(scores, lives):
        size = part.shape[0] // len(live)
        pieces.append([part[c * size : (c + 1) * size] for c in range(len(live))])
    peaks = [
        jnp.where(alive, jnp.max(piece, axis=0, keepdims=True), NEG_FILL)
        for row, live in zip(pieces, lives)
        for piece, alive in zip(row, live)
    ]
    peak = functools.reduce(jnp.maximum, peaks)
    shift = jnp.maximum(peak * TO_LOG2, FLOOR).astype(jnp.bfloat16).astype(jnp.float32)
    total = jnp.zeros((1, ROWS), jnp.float32)
    acc = jnp.zeros((HD, ROWS), jnp.float32)
    for row, live, value in zip(pieces, lives, values):
        expo = jnp.concatenate(
            [
                jnp.exp2(piece * TO_LOG2 - jnp.where(alive, shift, -NEG_FILL))
                for piece, alive in zip(row, live)
            ],
            axis=0,
        )
        total += jnp.sum(expo, axis=0, keepdims=True)
        acc += lax.dot_general(
            value, expo.astype(jnp.bfloat16), CONTRACT_FIRST, preferred_element_type=jnp.float32
        )
    return shift, total, acc


def write_packet(out_ref, shift, total, acc):
    high = total.astype(jnp.bfloat16).astype(jnp.float32)
    line = lax.broadcasted_iota(jnp.int32, (STATS, ROWS), 0)
    stats = jnp.where(line == 0, shift, jnp.where(line == 1, high, jnp.where(line == 2, total - high, 0.0)))
    out_ref[:HD, :] = acc.astype(jnp.bfloat16)
    out_ref[HD:, :] = stats.astype(jnp.bfloat16)


def merge_parts(parts):
    top = functools.reduce(jnp.maximum, [part[0] for part in parts])
    factors = [jnp.exp2(part[0] - top) for part in parts]
    total = sum(f * part[1] for f, part in zip(factors, parts))
    return top, total, sum(f * part[2] for f, part in zip(factors, parts))


def read_packet(ref):
    stats = ref[HD:, :].astype(jnp.float32)
    return stats[0:1], stats[1:2] + stats[2:3], ref[:HD, :].astype(jnp.float32)


def cached_scores(shift, me_ref, table_ref, rows, blocks):
    zo, xr = coordinates(me_ref)
    home = rem(zo + shift, NZ) * NX + xr
    scores, lives, values = [], [], []
    for k in (1, 2, 3, 0):
        owner = zo * NX + rem(xr - k, NX)
        both = blocks[k].reshape(CAP * BLK, 2 * HD)
        scores.append(
            lax.dot_general(both[:, :HD], rows, CONTRACT_LAST, preferred_element_type=jnp.float32)
        )
        lives.append([table_ref[home, 0, owner * CAP + c] >= 0 for c in range(CAP)])
        values.append(both[:, HD:])
    return scores, lives, values


def suffix_part(rows, both):
    scores = lax.dot_general(both[:, :HD], rows, CONTRACT_LAST, preferred_element_type=jnp.float32)
    key = lax.broadcasted_iota(jnp.int32, (SUF, ROWS), 0)
    token = lax.rem(lax.broadcasted_iota(jnp.int32, (SUF, ROWS), 1), SUF)
    return partial_sums([jnp.where(key <= token, scores, NEG_FILL)], [[True]], [both[:, HD:]])


def attend_kernel(chunk, shifts, has, *refs):
    refs = list(refs)
    take = lambda n: [refs.pop(0) for _ in range(n)]
    me_ref, table_ref, cache_ref, z_query_ref = take(4)
    arrived = take(NX - 1)
    own_refs = take(2 * has["suffix"])
    relayed = take(2 * has["relayed"])
    weight_ref = take(2)[0] if has["weight"] else None
    packet_refs = take(2 if has["relay"] else len(shifts))
    own_packet = take(1)[0] if has["suffix"] else None
    wide_ref = take(1)[0] if has["weight"] else None
    here, query_here, block_sem, query_sems, wide_sems = take(5)
    zo, _ = coordinates(me_ref)
    wide = []
    if has["weight"]:
        step = weight_ref.shape[0] // WIDE_PARTS
        for n in range(WIDE_PARTS):
            part = pl.ds(n * step, step)
            wide.append(
                pltpu.make_async_copy(weight_ref.at[part, :], wide_ref.at[part, :], wide_sems.at[n])
            )
            wide[-1].start()
    first = chunk.index(shifts[0])
    fetches = [
        pltpu.make_async_copy(
            z_query_ref.at[rem(zo + shift, NZ)], query_here.at[n], query_sems.at[n]
        )
        for n, shift in enumerate(shifts)
    ]
    for fetch in fetches:
        fetch.start()
    start_picks(shifts, 0, me_ref, table_ref, cache_ref, here, block_sem)
    if has["suffix"]:
        part = suffix_part(head_rows(own_refs[0][...]), own_refs[1][...])
        write_packet(own_packet, *part)
    for fetch in fetches:
        fetch.wait()
    wait_picks(shifts, cache_ref, here, block_sem)
    def scores_of(n):
        there = slice((first + n) * CAP, (first + n + 1) * CAP)
        blocks = [here[n * CAP : (n + 1) * CAP]] + [ref[there] for ref in arrived]
        return cached_scores(shifts[n], me_ref, table_ref, head_rows(query_here[n]), blocks)

    following = scores_of(0)
    for n, shift in enumerate(shifts):
        current = following
        if n + 1 < len(shifts):
            following = scores_of(n + 1)
        part = partial_sums(*current)
        if has["relay"]:
            out = {4: packet_refs[0].at[0], 3: packet_refs[0].at[1], 5: packet_refs[1]}[shift]
        else:
            out = packet_refs[n]
        if has["relayed"] and shift in (2, 1, 7):
            other = {2: relayed[0].at[0], 1: relayed[0].at[1], 7: relayed[1]}[shift]
            part = merge_parts([part, read_packet(other)])
        write_packet(out, *part)
    for copy in wide:
        copy.wait()


def attend(chunk, shifts, me, table, cache, z_queries, arrived, own=(), relay=False, relayed=(), weight=()):
    keys = len(shifts) * NX * CAP * BLK
    has = dict(suffix=bool(own), relay=relay, relayed=bool(relayed), weight=bool(weight))
    packet = jax.ShapeDtypeStruct((PACKET, ROWS), jnp.bfloat16)
    pair = jax.ShapeDtypeStruct((2, PACKET, ROWS), jnp.bfloat16)
    packets = ([pair, packet] if relay else [packet] * len(shifts)) + [packet] * bool(own)
    wide = [pltpu.VMEM(weight[0].shape, weight[0].dtype)] if weight else []
    outs = pl.pallas_call(
        functools.partial(attend_kernel, chunk, shifts, has),
        out_shape=packets + wide,
        in_specs=[IN_SMEM] * 2
        + [IN_HBM] * 2
        + [IN_VMEM] * (NX - 1 + len(own) + len(relayed))
        + [IN_HBM] * len(weight),
        out_specs=[IN_VMEM] * len(packets + wide),
        scratch_shapes=[
            pltpu.VMEM((len(shifts) * CAP, BLK, 2 * HD), cache.dtype),
            pltpu.VMEM((len(shifts), SUF, GROUP * HD), jnp.bfloat16),
            pltpu.SemaphoreType.DMA,
            pltpu.SemaphoreType.DMA((len(shifts),)),
            pltpu.SemaphoreType.DMA((WIDE_PARTS,)),
        ],
        compiler_params=pltpu.CompilerParams(vmem_limit_bytes=VMEM_LIMIT),
        cost_estimate=pl.CostEstimate(
            flops=4 * keys * ROWS * HD, bytes_accessed=4 * keys * HD, transcendentals=keys * ROWS
        ),
        name="attend_chunk",
    )(me, table, cache, z_queries, *arrived, *own, *relayed, *weight)
    return outs


def finish_kernel(core_ref, wide_ref, *rest):
    packet_refs, send_ref, keep_ref = rest[:-2], rest[-2], rest[-1]
    _, row_sum, summed = merge_parts([read_packet(ref) for ref in packet_refs])
    rows = (summed / row_sum).T.astype(jnp.bfloat16)
    attended = jnp.concatenate([rows[i * SUF : (i + 1) * SUF] for i in range(GROUP)], axis=1)
    partial = jnp.dot(attended, wide_ref[...], preferred_element_type=jnp.float32)
    groups = [partial[n * HEAD_ROWS : (n + 1) * HEAD_ROWS] for n in range(NY * CORES)]
    halves = [jnp.concatenate(groups[c::CORES], axis=0) for c in range(CORES)]
    first = core_ref[0] == 0
    send_ref[...] = jnp.where(first, halves[1], halves[0]).astype(jnp.bfloat16)
    keep_ref[...] = jnp.where(first, halves[0], halves[1])


def finish(core, wide, packets):
    half = (NY * HEAD_ROWS, wide.shape[1])
    return pl.pallas_call(
        finish_kernel,
        out_shape=[
            jax.ShapeDtypeStruct(half, jnp.bfloat16),
            jax.ShapeDtypeStruct(half, jnp.float32),
        ],
        in_specs=[IN_SMEM] + [IN_VMEM] * (1 + len(packets)),
        out_specs=[IN_VMEM] * 2,
        compiler_params=pltpu.CompilerParams(vmem_limit_bytes=VMEM_LIMIT),
        cost_estimate=pl.CostEstimate(
            flops=2 * SUF * wide.size, bytes_accessed=2 * wide.size, transcendentals=0
        ),
        name="merge_project",
    )(core, wide, *packets)


def x_permute(a, step):
    pairs = [(z * NX + x, z * NX + (x + step) % NX) for z in range(NZ) for x in range(NX)]
    return lax.ppermute(a, "store", pairs)


def z_permute(a, step):
    pairs = [(z * NX + x, ((z + step) % NZ) * NX + x) for z in range(NZ) for x in range(NX)]
    return lax.ppermute(a, "store", pairs)


def y_permute(a, step):
    pairs = [
        (y * CORES + c, ((y + step) % NY) * CORES + c) for y in range(NY) for c in range(CORES)
    ]
    return lax.ppermute(a, "head", pairs)


def core_swap(a):
    return lax.ppermute(a, "head", [(h, h ^ 1) for h in range(NY * CORES)])


def sum_heads(send, keep):
    y = lax.div(lax.axis_index("head"), CORES)
    both = (keep + core_swap(send).astype(jnp.float32)).reshape(NY, HEAD_ROWS, keep.shape[1])
    pick_y = lambda step: lax.dynamic_index_in_dim(both, rem(y + step, NY), 0, keepdims=False)
    arrived = [y_permute(pick_y(step).astype(jnp.bfloat16), step) for step in (2, 1, 3)]
    return (pick_y(0) + sum(a.astype(jnp.float32) for a in arrived)).astype(jnp.bfloat16)


def local(queries, suffix_kv, kv_cache, block_owner, block_slot, prefix_blocks, out_weight):
    store_count = lax.axis_size("store")
    me = lax.axis_index("store").astype(jnp.int32).reshape(1)
    wanted, copies = wanted_slots(prefix_blocks, block_owner, block_slot, queries, store_count)
    table = lax.all_to_all(wanted, "store", split_axis=0, concat_axis=0, tiled=True)
    cache = keep_in_hbm(kv_cache.reshape(kv_cache.shape[0], BLK, 2 * HD))
    suffix = suffix_kv.reshape(SUF, 2 * HD)
    far, near = CHUNKS
    away = near[:-1]
    over_x = lambda blocks: [x_permute(block, k) for k, block in enumerate(blocks, 1)]
    over_z = lambda shifts, parts: [z_permute(part, s) for s, part in zip(shifts, parts)]
    far_sent = pick_far(far, me, table, cache)
    far_blocks = over_x(far_sent)
    near_blocks = over_x(pick_near(near, me, table, cache))
    z_groups = [[z * NX + x for z in range(NZ)] for x in range(NX)]
    z_queries = keep_in_hbm(
        lax.all_to_all(
            copies, "store", split_axis=0, concat_axis=0, tiled=True, axis_index_groups=z_groups
        )
    )
    common = (me, table, cache, z_queries)
    plus, minus, own = attend(far, far, *common, far_blocks, own=(queries, suffix), relay=True)
    relayed = (z_permute(plus, RELAY), z_permute(minus, -RELAY))
    parts = attend(near, away, *common, near_blocks, relayed=relayed)
    packets = over_z(away, parts) + [own]
    home, wide = attend(
        near, near[-1:], *common, near_blocks, weight=(keep_in_hbm(out_weight), parts[0])
    )
    core = lax.rem(lax.axis_index("head"), CORES).astype(jnp.int32).reshape(1)
    return sum_heads(*finish(core, wide, packets + [home]))


def solution(mesh):
    in_specs = (
        P("store", "head"),
        P("store", "head", None),
        P("store", "head", None, None),
        P("store", None),
        P("store", None),
        P("store"),
        P("head", None),
    )
    out_specs = P(("store", "head"), None)
    return jax.shard_map(local, mesh=mesh, in_specs=in_specs, out_specs=out_specs, check_vma=False)
```
